128 devices in a mesh: dp: 16 (over y, x), seq: 8 (over z, core).
Axes of the slice: x: 4, y: 4, z: 4, core: 2. Of those that a mesh axis runs over, the one named last changes fastest.
Arguments:
- queries: bfloat16 [32768, 8192], P(('dp', 'seq')), may hold values from -60 to 60
- keys: bfloat16 [32768, 1024], P(('dp', 'seq')), may hold values from -60 to 60
- values: bfloat16 [32768, 1024], P(('dp', 'seq')), may hold values from -6 to 6
- plan: int32 [32768], P(('dp', 'seq')), may hold values from 0 to 32767, as said below
- segment_ids: int32 [32768], P(('dp', 'seq')), may hold values from 0 to 255, as said below
Outputs:
- attended: bfloat16 [32768, 8192], P(('dp', 'seq'))
The draws below stay inside these ranges and needn't reach their ends.
Inputs may be any that keep to these rules, and one draw needn't show every extreme that they name: `plan`: A permutation of the owner rows. The rows of one device go exactly 2 to each device (owner rows d * 256 to (d + 1) * 256 - 1 belong to device d), in random order among the device's rows. `segment_ids`: documents are runs of equal ids that never fall; every length is a multiple of 128; no document crosses a boundary of the aligned blocks of 2048 owner rows; one document fills a whole block.
All inputs are finite; a program needn't handle non-finite values.
Results may differ from the reference program's by a relative error of at most 0.0053.
Values may be sent and summed in bfloat16 or wider, within the bound.
No kernel may reach another device: no remote copies, remote signals or barrier semaphores. Data moves between devices by JAX's collectives and lax.ppermute only.
A program may use at most 128 MiB of HBM per device.

```python
import jax
import jax.numpy as jnp
from jax import lax

H = 64
KVH = 8
HD = 128
TOK_DEV = 256
TOKENS = 32768
GROUP = 2048


def make_plan(key):
    devices = TOKENS // TOK_DEV
    share = TOK_DEV // devices
    alpha = jax.random.permutation(jax.random.fold_in(key, 101), devices).astype(jnp.int32)
    beta = jax.random.permutation(jax.random.fold_in(key, 102), devices).astype(jnp.int32)
    gamma = jax.random.permutation(jax.random.fold_in(key, 103), devices).astype(jnp.int32)
    slots = jnp.arange(TOK_DEV, dtype=jnp.int32)
    blocks = slots // share
    target = alpha[(beta[:, None] + gamma[blocks][None, :]) % devices]
    owner_rows = target * TOK_DEV + slots[None, :]
    shuffle_keys = jax.random.split(jax.random.fold_in(key, 104), devices)
    shuffles = jax.vmap(lambda single: jax.random.permutation(single, TOK_DEV))(shuffle_keys).astype(jnp.int32)
    placed = jnp.take_along_axis(owner_rows, shuffles, axis=1)
    return placed.reshape(TOKENS).astype(jnp.int32)


def draw_plan(key, part):
    return make_plan(key)


def draw_segment_ids(key, part):
    unit = TOK_DEV // 2
    units = TOKENS // unit
    per_group = GROUP // unit
    groups = units // per_group
    places = jnp.arange(units, dtype=jnp.int32)
    inside = places % per_group
    rolls = jax.random.randint(jax.random.fold_in(key, 201), (units,), 0, 20).astype(jnp.int32)
    limit = jnp.where(inside % 2 == 1, 3, 9)
    cuts = jnp.where(rolls < limit, 1, 0).astype(jnp.int32)
    whole = jax.random.randint(jax.random.fold_in(key, 202), (), 0, groups).astype(jnp.int32)
    cuts = jnp.where(places // per_group == whole, 0, cuts)
    cuts = jnp.where(inside == 0, 1, cuts)
    cuts = jnp.where(places == units - 1, 1, cuts)
    labels = lax.cummax(jnp.where(cuts == 1, places, jnp.zeros_like(places)), axis=0)
    return jnp.repeat(labels, unit).astype(jnp.int32)


def draw_queries(key, part):
    base = jnp.clip(jax.random.normal(jax.random.fold_in(key, 402), (TOKENS, H * HD), jnp.float32), -6.0, 6.0)
    return base.astype(jnp.bfloat16)


def draw_keys(key, part):
    base = jnp.clip(jax.random.normal(jax.random.fold_in(key, 502), (TOKENS, KVH * HD), jnp.float32), -6.0, 6.0)
    return base.astype(jnp.bfloat16)


def block_levels(stream_key, extent, cuts, low, top_value):
    def one(position, parts):
        heights = jax.random.uniform(jax.random.fold_in(jax.random.fold_in(stream_key, 6), position), (parts,), jnp.float32, low / len(cuts), top_value / len(cuts))
        return jnp.repeat(jnp.exp(heights), extent[position] // parts).reshape((-1,) + (1,) * (len(extent) - position - 1))

    loudness = one(*cuts[0])
    for cut in cuts[1:]:
        loudness = loudness * one(*cut)
    return loudness


def scatter_about(stream_key, dims, deviation, most, cuts=(), kind=jnp.bfloat16):
    values = jax.random.normal(stream_key, dims, jnp.float32) * deviation
    if len(cuts) > 0:
        values = block_levels(stream_key, dims, cuts, -0.22, 0.18) * values
    return jnp.clip(values, min=-most, max=most).astype(kind)


def setup_inputs(seed: int = 0) -> dict:
    key_of = jax.random.split(jax.random.key(seed), 6)
    return {
        "queries": draw_queries(jax.random.fold_in(key_of[5], 71), 0),
        "keys": draw_keys(jax.random.fold_in(key_of[5], 71), 0),
        "values": scatter_about(key_of[2], (TOKENS, KVH * HD), 1.0, 6.0, ((0, 128),)),
        "plan": draw_plan(jax.random.fold_in(key_of[5], 71), 0),
        "segment_ids": draw_segment_ids(jax.random.fold_in(key_of[5], 71), 0),
    }


theta_base = 500000.0
tile_rows = 512


def doc_positions(segment_ids):
    places = jnp.arange(segment_ids.shape[0], dtype=jnp.int32)
    starts = jnp.concatenate([jnp.ones((1,), jnp.bool_), segment_ids[1:] != segment_ids[:-1]])
    first = lax.cummax(jnp.where(starts, places, jnp.zeros_like(places)), axis=0)
    return places - first


def rotate(source, positions):
    width = source.shape[-1]
    half = width // 2
    freqs = theta_base ** (-2.0 * jnp.arange(half, dtype=jnp.float32) / width)
    angles = positions.astype(jnp.float32)[:, None] * freqs[None, :]
    cosine = jnp.cos(angles)[:, None, :]
    sine = jnp.sin(angles)[:, None, :]
    floats = source.astype(jnp.float32)
    lower = floats[..., :half]
    upper = floats[..., half:]
    turned = jnp.concatenate([lower * cosine - upper * sine, upper * cosine + lower * sine], axis=-1)
    return turned.astype(jnp.bfloat16)


def masked_block(query_block, key_part, value_part, query_ids, key_ids, anchor):
    count = query_block.shape[0]
    reach = key_part.shape[0]
    scores = jnp.einsum("qkgd,tkd->kgqt", query_block.astype(jnp.float32), key_part.astype(jnp.float32)) * (HD ** -0.5)
    query_rows = anchor + jnp.arange(count, dtype=jnp.int32)
    key_rows = jnp.arange(reach, dtype=jnp.int32)
    allowed = (key_rows[None, :] <= query_rows[:, None]) & (key_ids[None, :] == query_ids[:, None])
    scores = jnp.where(allowed, scores, -jnp.inf)
    peak = jnp.max(scores, axis=-1, keepdims=True)
    weights = jnp.exp(scores - peak)
    totals = jnp.sum(weights, axis=-1)
    rounded = lax.optimization_barrier(weights.astype(jnp.bfloat16)).astype(jnp.float32)
    mixed = jnp.einsum("kgqt,tkd->kgqd", rounded, value_part.astype(jnp.float32))
    result = mixed / totals[..., None]
    return jnp.transpose(result, (2, 0, 1, 3)).astype(jnp.bfloat16)


def reference(queries, keys, values, plan, segment_ids):
    total = queries.shape[0]
    per_kv = H // KVH
    own_q = jnp.zeros_like(queries).at[plan].set(queries)
    own_k = jnp.zeros_like(keys).at[plan].set(keys)
    own_v = jnp.zeros_like(values).at[plan].set(values)
    positions = doc_positions(segment_ids)
    rot_q = rotate(own_q.reshape(total, H, HD), positions).reshape(total, KVH, per_kv, HD)
    rot_k = rotate(own_k.reshape(total, KVH, HD), positions)
    own_v = own_v.reshape(total, KVH, HD)

    def one_group(number):
        start = number * GROUP
        group_q = lax.dynamic_slice_in_dim(rot_q, start, GROUP, 0)
        group_k = lax.dynamic_slice_in_dim(rot_k, start, GROUP, 0)
        group_v = lax.dynamic_slice_in_dim(own_v, start, GROUP, 0)
        group_ids = lax.dynamic_slice_in_dim(segment_ids, start, GROUP, 0)
        pieces = []
        for block in range(GROUP // tile_rows):
            low = block * tile_rows
            high = low + tile_rows
            pieces.append(masked_block(group_q[low:high], group_k[:high], group_v[:high], group_ids[low:high], group_ids[:high], low))
        return jnp.concatenate(pieces, axis=0)

    outputs = lax.map(one_group, jnp.arange(total // GROUP, dtype=jnp.int32))
    own_out = outputs.reshape(total, H * HD)
    return own_out[plan]
```

```python
import functools

import jax
import jax.numpy as jnp
from jax import lax
from jax.experimental import pallas as pl
from jax.experimental.pallas import tpu as pltpu
from jax.sharding import PartitionSpec as P

H = 64
KVH = 8
HD = 128
ROWS = 256
AXES = ("dp", "seq")
SEQ = 8
GROUPS = 16
DEVICES = SEQ * GROUPS
PER = ROWS // GROUPS
GROUP = SEQ * ROWS
PER_KV = H // KVH
FIRST = 4
BIG = 1e30
theta_base = 500000.0
MIB = 1024 * 1024

f32 = jnp.float32
bf16 = jnp.bfloat16


def params(mib):
    return pltpu.CompilerParams(vmem_limit_bytes=mib * MIB)


def dot(a, b):
    return jnp.dot(a, b, preferred_element_type=f32)


def order_kernel(plan_ref, ids_ref, perm_ref, back_ref, note_ref):
    wide = jnp.broadcast_to(plan_ref[...].astype(f32), (ROWS, ROWS))
    tall = wide.T
    rank_row = jnp.sum((tall < wide).astype(f32), axis=0, keepdims=True).astype(jnp.int32)
    rank_col = jnp.sum((wide < tall).astype(f32), axis=1, keepdims=True).astype(jnp.int32)
    down = lax.broadcasted_iota(jnp.int32, (ROWS, ROWS), 0)
    along = lax.broadcasted_iota(jnp.int32, (ROWS, ROWS), 1)
    perm_ref[...] = (rank_row == down).astype(bf16)
    hit = rank_col == along
    back_ref[...] = hit.astype(bf16)
    ordered = jnp.sum(jnp.where(hit, tall, 0.0), axis=0, keepdims=True)
    note_ref[:, :ROWS] = ordered.astype(jnp.int32)
    lane = lax.broadcasted_iota(jnp.int32, (1, 128), 1)
    halves = ids_ref[...]
    note_ref[:, ROWS:] = jnp.where(lane < 64, halves[:, :1], halves[:, ROWS - 1 :])


def order_rows(plan, segment_ids):
    square = jax.ShapeDtypeStruct((ROWS, ROWS), bf16)
    return pl.pallas_call(
        order_kernel,
        out_shape=(square, square, jax.ShapeDtypeStruct((1, ROWS + 128), jnp.int32)),
        name="order_rows",
    )(plan.reshape(1, ROWS), segment_ids.reshape(1, ROWS))


def pack_kernel(perm_ref, *refs):
    out_ref = refs[-1]
    perm = perm_ref[...]
    at = 0
    for ref in refs[:-1]:
        width = ref.shape[1]
        moved = dot(perm, ref[...]).astype(bf16)
        out_ref[:, 0, :, at : at + width] = moved.reshape(GROUPS, PER, width)
        at += width


def pack(perm, parts):
    width = sum(w for _, w, _ in parts)
    specs = [pl.BlockSpec((ROWS, w), functools.partial(lambda f, h: (0, f(h)), f)) for _, w, f in parts]
    out = pl.pallas_call(
        pack_kernel,
        grid=(SEQ,),
        in_specs=[pl.BlockSpec((ROWS, ROWS), lambda h: (0, 0))] + specs,
        out_specs=pl.BlockSpec((GROUPS, 1, PER, width), lambda h: (0, h, 0, 0)),
        out_shape=jax.ShapeDtypeStruct((GROUPS, SEQ, PER, width), bf16),
        compiler_params=params(24),
        cost_estimate=pl.CostEstimate(
            flops=2 * ROWS * ROWS * SEQ * width,
            bytes_accessed=4 * ROWS * SEQ * width,
            transcendentals=0,
        ),
        name="pack_rows",
    )(perm, *[a for a, _, _ in parts])
    return out.reshape(DEVICES, PER, width)


def unpack_kernel(back_ref, in_ref, *refs):
    out_ref = refs[-1]
    out_ref[...] = dot(back_ref[...], in_ref[:, 0].reshape(ROWS, -1)).astype(bf16)


def unpack(back, home, place, into):
    width = home.shape[-1]
    aliases = {} if into is None else {2: 0}
    more = [] if into is None else [into]
    return pl.pallas_call(
        unpack_kernel,
        grid=(SEQ,),
        in_specs=[
            pl.BlockSpec((ROWS, ROWS), lambda h: (0, 0)),
            pl.BlockSpec((GROUPS, 1, PER, width), lambda h: (0, h, 0, 0)),
        ]
        + [pl.BlockSpec(memory_space=pl.ANY) for _ in more],
        out_specs=pl.BlockSpec((ROWS, width), lambda h: (0, place(h))),
        out_shape=jax.ShapeDtypeStruct((ROWS, H * HD), bf16),
        input_output_aliases=aliases,
        compiler_params=params(24),
        cost_estimate=pl.CostEstimate(
            flops=2 * ROWS * ROWS * SEQ * width,
            bytes_accessed=4 * ROWS * SEQ * width,
            transcendentals=0,
        ),
        name="unpack_rows",
    )(back, home.reshape(GROUPS, SEQ, PER, width), *more)


def tables(notes):
    group = lax.axis_index("dp")
    rows = lax.dynamic_slice(notes, (0, PER * group), (DEVICES, PER)) - GROUP * group
    units = lax.dynamic_slice(notes, (SEQ * group, ROWS), (SEQ, 128))[:, ::64].reshape(16)
    begin = jnp.sum((units[None, :] < units[:, None]).astype(jnp.int32), axis=1)
    number = jnp.arange(16, dtype=jnp.int32)

    rows = rows.reshape(8, 16, 8, 2)
    by_chunk = jnp.transpose(rows, (0, 2, 1, 3)).reshape(GROUP)
    by_block = jnp.transpose(rows, (2, 0, 1, 3)).reshape(GROUP)

    def begin_of(places):
        return jnp.sum(jnp.where((places >> 7)[:, None] == number[None, :], begin[None, :], 0), axis=1)

    position = (by_chunk - 128 * begin_of(by_chunk)).astype(f32)
    freqs = theta_base ** (-2.0 * jnp.arange(HD // 2, dtype=f32) / HD)
    angles = position[:, None] * freqs[None, :]
    cosine = jnp.cos(angles)
    sine = jnp.sin(angles)
    turn_c = jnp.concatenate([cosine, cosine], axis=1)
    turn_s = jnp.concatenate([-sine, sine], axis=1)

    lanes = jnp.arange(HD, dtype=jnp.int32)
    q_mark = jnp.where(lanes[None, :] < begin_of(by_block)[:, None], -BIG, 0.0).astype(bf16)
    k_mark = ((by_block >> 7)[None, :] == lanes[:, None]).astype(bf16)
    blocks = by_block.reshape(SEQ, ROWS)
    causal = jnp.where(blocks[:, None, :] <= blocks[:, :, None], 0.0, -BIG).astype(bf16)
    return turn_c, turn_s, q_mark, k_mark, causal


def attend_kernel(
    xq_ref, xk_ref, xv_ref, turn_c_ref, turn_s_ref, q_mark_ref, k_mark_ref, causal_ref,
    out_ref, perm_ref, back_ref, kt_ref, vv_ref, qs_ref, os_ref,
):
    factor = (HD ** -0.5) * 1.4426950408889634

    def settle(x_ref, chunk, turn):
        moved = dot(perm_ref[...], x_ref[16 * chunk : 16 * chunk + 16].reshape(ROWS, HD))
        if turn:
            here = slice(chunk * ROWS, chunk * ROWS + ROWS)
            moved = moved * turn_c_ref[here, :] + pltpu.roll(moved, HD // 2, 1) * turn_s_ref[here, :]
        return moved.astype(bf16)

    def spread(target, x_ref, turn):
        for chunk in range(8):
            moved = settle(x_ref, chunk, turn)
            for s in range(SEQ):
                at = s * ROWS + chunk * 32
                target[at : at + 32, :HD] = moved[s * 32 : s * 32 + 32]

    @pl.when(pl.program_id(0) == 0)
    def _():
        down = lax.broadcasted_iota(jnp.int32, (ROWS, ROWS), 0)
        along = lax.broadcasted_iota(jnp.int32, (ROWS, ROWS), 1)

        def source(j):
            return ((j >> 1) & 15) * 16 + 2 * (j >> 5) + (j & 1)

        perm_ref[...] = (source(down) == along).astype(bf16)
        back_ref[...] = (source(along) == down).astype(bf16)
        spread(vv_ref, xk_ref, True)
        for s in range(SEQ):
            here = slice(s * ROWS, s * ROWS + ROWS)
            kt_ref[:HD, here] = vv_ref[here, :HD].astype(f32).T.astype(bf16)
        kt_ref[HD:, :] = k_mark_ref[...]
        spread(vv_ref, xv_ref, False)
        vv_ref[:, HD:] = jnp.ones((GROUP, HD), bf16)
        qs_ref[:, HD:] = q_mark_ref[...]

    spread(qs_ref, xq_ref, True)
    for s in range(SEQ):
        here = slice(s * ROWS, s * ROWS + ROWS)
        diagonal = dot(qs_ref[here, :], kt_ref[:, here]) + causal_ref[here, :].astype(f32)
        peak = jnp.max(diagonal, axis=1, keepdims=True)
        if s > 0:
            before = dot(qs_ref[here, :], kt_ref[:, : s * ROWS])
            peak = jnp.maximum(peak, jnp.max(before, axis=1, keepdims=True))
            weight = jnp.exp2((before - peak) * factor).astype(bf16)
            mixed = dot(weight, vv_ref[: s * ROWS, :])
        weight = jnp.exp2((diagonal - peak) * factor).astype(bf16)
        last = dot(weight, vv_ref[here, :])
        mixed = last if s == 0 else mixed + last
        os_ref[here, :] = (mixed[:, :HD] / mixed[:, HD:]).astype(bf16)
    for chunk in range(8):
        rows = [os_ref[s * ROWS + chunk * 32 : s * ROWS + chunk * 32 + 32, :] for s in range(SEQ)]
        moved = dot(back_ref[...], jnp.concatenate(rows, axis=0)).astype(bf16)
        out_ref[16 * chunk : 16 * chunk + 16] = moved.reshape(16, PER, HD)


def attend(heads, q_from, q_at, kv_from, tabs):
    turn_c, turn_s, q_mark, k_mark, causal = tabs

    def block(at):
        return pl.BlockSpec((DEVICES, PER, HD), at)

    def whole(shape):
        return pl.BlockSpec(shape, lambda h: (0, 0))

    pairs = heads * GROUP * GROUP * 36 // 64
    return pl.pallas_call(
        attend_kernel,
        grid=(heads,),
        in_specs=[
            block(lambda h: (0, 0, q_at + h)),
            block(lambda h: (0, 0, 0)),
            block(lambda h: (0, 0, 1)),
            whole((GROUP, HD)),
            whole((GROUP, HD)),
            whole((GROUP, HD)),
            whole((HD, GROUP)),
            whole((GROUP, ROWS)),
        ],
        out_specs=block(lambda h: (0, 0, h)),
        out_shape=jax.ShapeDtypeStruct((DEVICES, PER, heads * HD), bf16),
        scratch_shapes=[
            pltpu.VMEM((ROWS, ROWS), bf16),
            pltpu.VMEM((ROWS, ROWS), bf16),
            pltpu.VMEM((2 * HD, GROUP), bf16),
            pltpu.VMEM((GROUP, 2 * HD), bf16),
            pltpu.VMEM((GROUP, 2 * HD), bf16),
            pltpu.VMEM((GROUP, HD), bf16),
        ],
        compiler_params=params(40),
        cost_estimate=pl.CostEstimate(
            flops=pairs * 2 * 2 * 256,
            bytes_accessed=heads * GROUP * HD * 4 + GROUP * HD * 16,
            transcendentals=pairs,
        ),
        name="attend",
    )(q_from, kv_from, kv_from, turn_c, turn_s, q_mark, k_mark, causal.reshape(GROUP, ROWS))


def exchange(x):
    return lax.all_to_all(x, AXES, split_axis=0, concat_axis=0, tiled=True)


def per_device(queries, keys, values, plan, segment_ids):
    perm, back, note = order_rows(plan, segment_ids)
    notes = lax.all_gather(note, AXES, axis=0, tiled=True)
    half = FIRST * HD
    send_0 = pack(perm, [(keys, HD, lambda h: h), (values, HD, lambda h: h), (queries, half, lambda h: 2 * h)])
    send_1 = pack(perm, [(queries, half, lambda h: 2 * h + 1)])
    got_0 = exchange(send_0)
    got_1 = exchange(send_1)
    tabs = tables(notes)
    out_0 = attend(FIRST, got_0, 2, got_0, tabs)
    home_0 = exchange(out_0)
    out_1 = attend(FIRST, got_1, 0, got_0, tabs)
    home_1 = exchange(out_1)
    partly = unpack(back, home_0, lambda h: 2 * h, None)
    return unpack(back, home_1, lambda h: 2 * h + 1, partly)


def solution(mesh):
    return jax.shard_map(
        per_device,
        mesh=mesh,
        in_specs=(
            P(AXES, None),
            P(AXES, None),
            P(AXES, None),
            P(AXES),
            P(AXES),
        ),
        out_specs=P(AXES, None),
        check_vma=False,
    )
```

```python
import functools

import jax
import jax.numpy as jnp
import numpy as np
from jax import lax
from jax.experimental import pallas as pl
from jax.experimental.pallas import tpu as pltpu
from jax.sharding import Mesh
from jax.sharding import PartitionSpec as P

H = 64
KVH = 8
HD = 128
ROWS = 256
SEQ = 8
GROUPS = 16
COLS = SEQ // 2
CHIPS = GROUPS * COLS
DEVICES = 2 * CHIPS
PER = ROWS // GROUPS
GROUP = SEQ * ROWS
PER_KV = H // KVH
CHUNKS = GROUP // ROWS
PART = 4
NOTE = 8
WIDE = PART * HD
BIG = 1e30
theta_base = 500000.0
MIB = 1024 * 1024

FLAT = ("dp", "z", "core")
CHIP_AXES = ("dp", "z")

f32 = jnp.float32
bf16 = jnp.bfloat16


def params(mib):
    return pltpu.CompilerParams(vmem_limit_bytes=mib * MIB)


def dot(a, b):
    return jnp.dot(a, b, preferred_element_type=f32)


def iota(shape, axis):
    return lax.broadcasted_iota(jnp.int32, shape, axis)


def order(plan_ref, ids_ref, perm_ref, back_ref):
    square = (ROWS, ROWS)
    wide = jnp.broadcast_to(plan_ref[...].astype(f32), square)
    tall = wide.T
    rank_row = jnp.sum((tall < wide).astype(f32), axis=0, keepdims=True).astype(jnp.int32)
    rank_col = jnp.sum((wide < tall).astype(f32), axis=1, keepdims=True).astype(jnp.int32)
    hit = rank_row == iota(square, 0)
    perm_ref[...] = hit.astype(bf16)
    back_ref[...] = (rank_col == iota(square, 1)).astype(bf16)
    ordered = jnp.sum(jnp.where(hit, wide, 0.0), axis=1, keepdims=True).astype(jnp.int32)
    place = (ordered & (ROWS - 1)).astype(f32)
    tall_shape = (ROWS, HD)
    laid = jnp.where((iota(tall_shape, 0) & (PER - 1)) == iota(tall_shape, 1), place, 0.0).astype(bf16)
    flat = (GROUPS * NOTE, ROWS)
    pick = ((iota(flat, 0) >> 3) == (iota(flat, 1) >> 4)).astype(bf16)
    lane = iota((GROUPS * NOTE, HD), 1)
    ids = ids_ref[...].astype(f32)
    note = jnp.where(lane == PER, ids[:, :1], dot(pick, laid))
    return jnp.where(lane == PER + 1, ids[:, ROWS - 1 :], note).astype(bf16)


def lanes(start, width):
    return pl.ds(pl.multiple_of(start, HD), width)


def start(copies):
    for copy in copies:
        copy.start()
    return copies


def wait(copies):
    for copy in copies:
        copy.wait()


def first_pack_kernel(
    plan_ref, ids_ref, k_ref, v_ref, q_ref, out_ref, perm_out, back_out,
    plan_in, ids_in, buffer, built, perm_ref, back_ref, sems, more_sems,
):
    early = start([
        pltpu.make_async_copy(plan_ref, plan_in, more_sems.at[0]),
        pltpu.make_async_copy(ids_ref, ids_in, more_sems.at[1]),
    ])
    copies = []
    for slot in range(SEQ):
        places = (
            (k_ref, slot * HD, 0, HD),
            (v_ref, slot * HD, HD, HD),
            (q_ref, slot * PER_KV * HD, 2 * HD, WIDE),
        )
        copies.append(start([
            pltpu.make_async_copy(
                ref.at[:, pl.ds(here, width)], buffer.at[slot, :, pl.ds(there, width)], sems.at[number, slot]
            )
            for number, (ref, here, there, width) in enumerate(places)
        ]))
    wait(early)
    note = order(plan_in, ids_in, perm_ref, back_ref).reshape(GROUPS, NOTE, HD)
    leaving = start([
        pltpu.make_async_copy(perm_ref, perm_out, more_sems.at[2]),
        pltpu.make_async_copy(back_ref, back_out, more_sems.at[3]),
    ])
    length = (PART + 2) * PER
    for z in range(COLS):
        for c in range(2):
            built[2 * z + c, :, length:, :] = note
    for low in range(0, SEQ, 4):
        for slot in range(low, low + 4):
            wait(copies[slot])
        for slot in range(low, low + 4):
            moved = dot(perm_ref[...], buffer[slot]).astype(bf16)
            for j in range(PART + 2):
                built[slot, :, j * PER : j * PER + PER, :] = moved[:, j * HD : j * HD + HD].reshape(GROUPS, PER, HD)
            leaving += start([pltpu.make_async_copy(built.at[slot], out_ref.at[:, slot], sems.at[3, slot])])
    wait(leaving)


def second_pack_kernel(core_ref, perm_ref, q_ref, out_ref, perm_in, buffer, built, sems, more_sems):
    early = start([pltpu.make_async_copy(perm_ref, perm_in, more_sems.at[0])])
    copies = []
    for z in range(COLS):
        for r in range(2):
            head = 2 * z + (r ^ core_ref[0])
            slot = 2 * z + r
            copies += start([
                pltpu.make_async_copy(
                    q_ref.at[:, lanes(head * (PER_KV * HD) + WIDE, WIDE)], buffer.at[slot], sems.at[0, slot]
                )
            ])
    wait(early)
    leaving = []
    for low in range(0, SEQ, 4):
        wait(copies[low : low + 4])
        for slot in range(low, low + 4):
            moved = dot(perm_in[...], buffer[slot]).astype(bf16)
            for j in range(PART):
                built[slot, :, j * PER : j * PER + PER, :] = moved[:, j * HD : j * HD + HD].reshape(GROUPS, PER, HD)
            z, r = divmod(slot, 2)
            rows = pl.ds(r * PART * PER, PART * PER)
            leaving += start([pltpu.make_async_copy(built.at[slot], out_ref.at[:, z, rows], sems.at[1, slot])])
    wait(leaving)


def lanes(first, width):
    return pl.ds(pl.multiple_of(first, HD), width)


def anywhere():
    return pl.BlockSpec(memory_space=pl.ANY)


def smem():
    return pl.BlockSpec(memory_space=pltpu.SMEM)


def vmem():
    return pl.BlockSpec(memory_space=pltpu.VMEM)


def work(flops, moved, transcendentals=0):
    return pl.CostEstimate(flops=flops, bytes_accessed=moved, transcendentals=transcendentals)


def first_pack(plan, segment_ids, keys, values, queries):
    length = (PART + 2) * PER + NOTE
    square = (ROWS, ROWS)
    out, perm, back = pl.pallas_call(
        first_pack_kernel,
        in_specs=[anywhere()] * 5,
        out_specs=[anywhere()] * 3,
        out_shape=(
            jax.ShapeDtypeStruct((GROUPS, SEQ, length, HD), bf16),
            jax.ShapeDtypeStruct(square, bf16),
            jax.ShapeDtypeStruct(square, bf16),
        ),
        scratch_shapes=[
            pltpu.VMEM((1, ROWS), jnp.int32),
            pltpu.VMEM((1, ROWS), jnp.int32),
            pltpu.VMEM((SEQ, ROWS, (PART + 2) * HD), bf16),
            pltpu.VMEM((SEQ, GROUPS, length, HD), bf16),
            pltpu.VMEM(square, bf16),
            pltpu.VMEM(square, bf16),
            pltpu.SemaphoreType.DMA((4, SEQ)),
            pltpu.SemaphoreType.DMA((4,)),
        ],
        compiler_params=params(60),
        cost_estimate=work(2 * ROWS * ROWS * SEQ * 768, 4 * ROWS * SEQ * 768),
        name="first_pack",
    )(plan.reshape(1, ROWS), segment_ids.reshape(1, ROWS), keys, values, queries)
    return out.reshape(DEVICES, length, HD), perm, back


def second_pack(core, perm, queries):
    length = 2 * PART * PER
    out = pl.pallas_call(
        second_pack_kernel,
        in_specs=[smem(), anywhere(), anywhere()],
        out_specs=anywhere(),
        out_shape=jax.ShapeDtypeStruct((GROUPS, COLS, length, HD), bf16),
        scratch_shapes=[
            pltpu.VMEM((ROWS, ROWS), bf16),
            pltpu.VMEM((SEQ, ROWS, WIDE), bf16),
            pltpu.VMEM((SEQ, GROUPS, PART * PER, HD), bf16),
            pltpu.SemaphoreType.DMA((2, SEQ)),
            pltpu.SemaphoreType.DMA((1,)),
        ],
        compiler_params=params(60),
        cost_estimate=work(2 * ROWS * ROWS * SEQ * WIDE, 4 * ROWS * SEQ * WIDE),
        name="second_pack",
    )(core, perm, queries)
    return out.reshape(CHIPS, length, HD)


def unpack_kernel(part, core_ref, back_ref, *refs):
    sources = refs[:2]
    out_ref, back_in, buffer, built, sems, more_sems = refs[-6:]
    early = start([pltpu.make_async_copy(back_ref, back_in, more_sems.at[0])])
    arriving, leaving = [], []
    for r in range(2):
        for z in range(COLS):
            slot = r * COLS + z
            arriving += start([pltpu.make_async_copy(sources[r].at[:, z, r], buffer.at[slot], sems.at[0, slot])])
    wait(early)
    for r in range(2):
        wait(arriving[r * COLS : r * COLS + COLS])
        for z in range(COLS):
            slot = r * COLS + z
            heads = [buffer[slot, :, j].reshape(ROWS, HD) for j in range(PART)]
            built[slot] = dot(back_in[...], jnp.concatenate(heads, axis=1)).astype(bf16)
            here = lanes((2 * z + (r ^ core_ref[0])) * (PER_KV * HD) + part * WIDE, WIDE)
            leaving += start([pltpu.make_async_copy(built.at[slot], out_ref.at[:, here], sems.at[1, slot])])
    wait(leaving)


def unpack(core, back, homes, part, into):
    more = [] if into is None else [into]
    return pl.pallas_call(
        functools.partial(unpack_kernel, part),
        in_specs=[smem()] + [anywhere()] * (3 + len(more)),
        out_specs=anywhere(),
        out_shape=jax.ShapeDtypeStruct((ROWS, H * HD), bf16),
        scratch_shapes=[
            pltpu.VMEM((ROWS, ROWS), bf16),
            pltpu.VMEM((SEQ, GROUPS, PART, PER, HD), bf16),
            pltpu.VMEM((SEQ, ROWS, WIDE), bf16),
            pltpu.SemaphoreType.DMA((2, SEQ)),
            pltpu.SemaphoreType.DMA((1,)),
        ],
        input_output_aliases={} if into is None else {4: 0},
        compiler_params=params(60),
        cost_estimate=work(2 * ROWS * ROWS * SEQ * WIDE, 4 * ROWS * SEQ * WIDE),
        name="unpack_rows",
    )(core, back, *[home.reshape(GROUPS, COLS, 2, PART, PER, HD) for home in homes], *more)


def turn_table():
    freqs = np.float32(theta_base) ** (np.float32(-2.0) * np.arange(HD // 2, dtype=np.float32) / np.float32(HD))
    freqs = freqs.astype(np.float64)
    low = np.arange(HD, dtype=np.float64)[:, None] * freqs[None, :]
    table = np.concatenate([np.cos(low), np.sin(low)], axis=1)
    terms = []
    for _ in range(3):
        term = table.astype(jnp.bfloat16)
        terms.append(term)
        table = table - term.astype(np.float64)
    high = 128.0 * np.arange(16, dtype=np.float64)[:, None] * freqs[None, :]
    c, s = np.cos(high), np.sin(high)
    tops = np.stack([np.concatenate(pair, axis=1) for pair in ((c, -s), (-s, c), (-c, s))])
    return np.concatenate(terms, axis=1), tops.astype(np.float32)


def source(j):
    return ((j >> 1) & 15) * 16 + 2 * (j >> 5) + (j & 1)


def chunk_of(x_ref, chunk, number):
    side, at = divmod(chunk, CHUNKS // 2)
    return x_ref[side, 16 * at : 16 * at + 16, number * PER : number * PER + PER].reshape(ROWS, HD)


def settle():
    square = (ROWS, ROWS)
    return (source(iota(square, 0)) == iota(square, 1)).astype(bf16)


def unsettle():
    square = (ROWS, ROWS)
    return (source(iota(square, 1)) == iota(square, 0)).astype(bf16)


def prepare(begin_ref, x_ref, note_ref, low_ref, tops_ref, tabs, place_ref):
    turn_c_ref, turn_s_ref, q_mark_ref, kt_ref, vv_ref, causal_ref = tabs
    perm = settle()
    strip = (ROWS, 16)
    loader = (((iota(strip, 0) >> 1) & 15) == iota(strip, 1)).astype(bf16)
    wide = (ROWS, HD)
    row, lane = iota(wide, 0), iota(wide, 1)
    slot = lane == 2 * (row >> 5) + (row & 1)
    ones = jnp.ones((HD, HD), bf16)
    lane = iota((32, HD), 1)
    for chunk in range(CHUNKS):
        spread = dot(loader, note_ref[16 * chunk : 16 * chunk + 16, :].astype(bf16))
        place = dot(jnp.where(slot, spread, 0.0).astype(bf16), ones)
        low = (place.astype(jnp.int32) & (HD - 1)) == iota(wide, 1)
        parts = dot(low.astype(bf16), low_ref[...])
        here = parts[:, :HD] + (parts[:, HD : 2 * HD] + parts[:, 2 * HD :])
        swapped = pltpu.roll(here, HD // 2, 1)
        both = dot(perm, jnp.concatenate([chunk_of(x_ref, chunk, 0), chunk_of(x_ref, chunk, 1)], axis=1))
        keys, values = both[:, :HD], both[:, HD:].astype(bf16)
        keys_swapped = pltpu.roll(keys, HD // 2, 1)
        for s in range(SEQ):
            piece = slice(s * 32, s * 32 + 32)
            at = slice(s * ROWS + chunk * 32, s * ROWS + chunk * 32 + 32)
            same = slice(chunk * ROWS + s * 32, chunk * ROWS + s * 32 + 32)
            mine = place[piece, :]
            place_ref[at, :] = mine
            first = mine < float(HD)
            begins = begin_ref[2 * s], begin_ref[2 * s + 1]
            gaps = 2 * s - begins[0], 2 * s + 1 - begins[1]
            top = [jnp.where(first, tops_ref[i, pl.ds(gaps[0], 1), :], tops_ref[i, pl.ds(gaps[1], 1), :]) for i in range(3)]
            turn_c = here[piece, :] * top[0] + swapped[piece, :] * top[1]
            turn_s = here[piece, :] * top[1] + swapped[piece, :] * top[2]
            turn_c_ref[same, :] = turn_c
            turn_s_ref[same, :] = turn_s
            q_mark_ref[at, :] = jnp.where(lane < jnp.where(first, begins[0], begins[1]), -BIG, 0.0).astype(bf16)
            turned = keys[piece, :] * turn_c + keys_swapped[piece, :] * turn_s
            vv_ref[at, HD:] = turned.astype(bf16)
            vv_ref[at, :HD] = values[piece, :]
    for s in range(SEQ):
        at = slice(s * ROWS, s * ROWS + ROWS)
        kt_ref[:HD, at] = vv_ref[at, HD:].astype(f32).T.astype(bf16)
        across = place_ref[at, :].T
        unit = jnp.where(across < float(HD), 2 * s, 2 * s + 1)
        kt_ref[HD:, at] = (unit == iota((HD, ROWS), 0)).astype(bf16)
        down = jnp.concatenate([place_ref[at, :], place_ref[at, :]], axis=1)
        causal_ref[at, :] = jnp.where(across[:1, :] <= down, 0.0, -BIG)
    vv_ref[:, HD:] = jnp.ones((GROUP, HD), bf16)


def take_queries(x_ref, first, tabs, qs_ref):
    turn_c_ref, turn_s_ref, q_mark_ref = tabs[:3]
    perm = settle()
    for chunk in range(CHUNKS):
        moved = dot(perm, jnp.concatenate([chunk_of(x_ref, chunk, first + h) for h in range(PART)], axis=1))
        same = slice(chunk * ROWS, chunk * ROWS + ROWS)
        turn_c, turn_s = turn_c_ref[same, :], turn_s_ref[same, :]
        for h in range(PART):
            one = moved[:, h * HD : h * HD + HD]
            one = (one * turn_c + pltpu.roll(one, HD // 2, 1) * turn_s).astype(bf16)
            for s in range(SEQ):
                at = h * ROWS + chunk * 32
                qs_ref[s, at : at + 32, :HD] = one[s * 32 : s * 32 + 32]
    for s in range(SEQ):
        for h in range(PART):
            qs_ref[s, h * ROWS : h * ROWS + ROWS, HD:] = q_mark_ref[s * ROWS : s * ROWS + ROWS, :]


def attend_blocks(tabs, qs_ref, os_ref):
    kt_ref, vv_ref, causal_ref = tabs[3:]
    factor = (HD ** -0.5) * 1.4426950408889634
    for s in range(SEQ):
        here = slice(s * ROWS, s * ROWS + ROWS)
        for h in range(PART):
            rows = slice(h * ROWS, h * ROWS + ROWS)
            block = qs_ref[s, rows, :]
            diagonal = dot(block, kt_ref[:, here]) + causal_ref[here, :]
            peak = jnp.max(diagonal, axis=1, keepdims=True)
            if s > 0:
                before = dot(block, kt_ref[:, : s * ROWS])
                peak = jnp.maximum(peak, jnp.max(before, axis=1, keepdims=True))
            weight = jnp.exp2((diagonal - peak) * factor).astype(bf16)
            if s > 0:
                weight = jnp.concatenate([jnp.exp2((before - peak) * factor).astype(bf16), weight], axis=1)
            mixed = dot(weight, vv_ref[: s * ROWS + ROWS, :])
            os_ref[s, rows, :] = (mixed[:, :HD] / mixed[:, HD:]).astype(bf16)


def give_back(os_ref, built, out_ref, sems, core=0):
    perm = unsettle()
    leaving = []
    for chunk in range(CHUNKS):
        heads = []
        for h in range(PART):
            at = h * ROWS + chunk * 32
            heads.append(jnp.concatenate([os_ref[s, at : at + 32, :] for s in range(SEQ)], axis=0))
        moved = dot(perm, jnp.concatenate(heads, axis=1)).astype(bf16)
        side, at = divmod(chunk, CHUNKS // 2)
        for h in range(PART):
            built[chunk, :, h] = moved[:, h * HD : h * HD + HD].reshape(16, PER, HD)
        leaving.append(pltpu.make_async_copy(built.at[chunk], out_ref.at[16 * at : 16 * at + 16, side ^ core], sems.at[chunk]))
        leaving[-1].start()
    return leaving


def first_attend_kernel(
    core_ref, begin_ref, note_ref, low_ref, tops_ref, got_ref, out_ref, *refs,
):
    tabs_out, (x_ref, place_ref, qs_ref, os_ref, built), tabs = refs[:6], refs[6:11], refs[11:17]
    in_sems, tab_sems, out_sems = refs[17:]
    length = (PART + 2) * PER
    arriving = []
    for low, high in ((0, 2 * PER), (2 * PER, length)):
        for side in range(2):
            here = got_ref.at[:, side ^ core_ref[0], low:high]
            arriving += start([pltpu.make_async_copy(here, x_ref.at[side, :, low:high], in_sems.at[len(arriving)])])
    arriving[0].wait()
    arriving[1].wait()
    prepare(begin_ref, x_ref, note_ref, low_ref, tops_ref, tabs, place_ref)
    leaving = []
    for number in range(6):
        leaving.append(pltpu.make_async_copy(tabs[number], tabs_out[number], tab_sems.at[number]))
        leaving[-1].start()
    arriving[2].wait()
    arriving[3].wait()
    take_queries(x_ref, 2, tabs, qs_ref)
    attend_blocks(tabs, qs_ref, os_ref)
    leaving += give_back(os_ref, built, out_ref, out_sems)
    for copy in leaving:
        copy.wait()


def second_attend_kernel(core_ref, own_ref, other_ref, *refs):
    tabs_in, out_ref, (x_ref, qs_ref, os_ref, built), tabs = refs[:6], refs[6], refs[7:11], refs[11:17]
    in_sems, tab_sems, out_sems = refs[17:]
    length = PART * PER
    arriving = []
    for side, ref in enumerate((own_ref, other_ref)):
        rows = slice(side * length, side * length + length)
        arriving.append(pltpu.make_async_copy(ref.at[:, rows], x_ref.at[side], in_sems.at[side]))
    for number in range(6):
        arriving.append(pltpu.make_async_copy(tabs_in[number], tabs[number], tab_sems.at[number]))
    for copy in arriving:
        copy.start()
    for copy in arriving[:5]:
        copy.wait()
    take_queries(x_ref, 0, tabs, qs_ref)
    for copy in arriving[5:]:
        copy.wait()
    attend_blocks(tabs, qs_ref, os_ref)
    wait(give_back(os_ref, built, out_ref, out_sems, core_ref[0]))


TABS = (
    ((GROUP, HD), f32),
    ((GROUP, HD), f32),
    ((GROUP, HD), bf16),
    ((2 * HD, GROUP), bf16),
    ((GROUP, 2 * HD), bf16),
    ((GROUP, ROWS), f32),
)
OUT = jax.ShapeDtypeStruct((CHIPS, 2, PART, PER, HD), bf16)


def attend_scratch(heads, with_place):
    place = [pltpu.VMEM((GROUP, HD), f32)] if with_place else []
    return [
        pltpu.VMEM((2, CHIPS, heads * PER, HD), bf16),
        *place,
        pltpu.VMEM((SEQ, PART * ROWS, 2 * HD), bf16),
        pltpu.VMEM((SEQ, PART * ROWS, HD), bf16),
        pltpu.VMEM((CHUNKS, 16, PART, PER, HD), bf16),
        *[pltpu.VMEM(shape, dtype) for shape, dtype in TABS],
        pltpu.SemaphoreType.DMA((4,)),
        pltpu.SemaphoreType.DMA((6,)),
        pltpu.SemaphoreType.DMA((CHUNKS,)),
    ]


def attend_work():
    pairs = PART * GROUP * GROUP * 36 // 64
    return work(pairs * 4 * 256, 16 * MIB, pairs)


def first_attend(core, begin, note, got):
    low, tops = turn_table()
    out, *tabs = pl.pallas_call(
        first_attend_kernel,
        in_specs=[smem(), smem(), vmem(), vmem(), vmem(), anywhere()],
        out_specs=[anywhere()] * 7,
        out_shape=[OUT] + [jax.ShapeDtypeStruct(shape, dtype) for shape, dtype in TABS],
        scratch_shapes=attend_scratch(PART + 2, True),
        compiler_params=params(60),
        cost_estimate=attend_work(),
        name="first_attend",
    )(core, begin, note, jnp.asarray(low), jnp.asarray(tops), got)
    return out, tabs


def second_attend(core, own, other, tabs):
    return pl.pallas_call(
        second_attend_kernel,
        in_specs=[smem()] + [anywhere()] * 8,
        out_specs=anywhere(),
        out_shape=OUT,
        scratch_shapes=attend_scratch(PART, False),
        compiler_params=params(60),
        cost_estimate=attend_work(),
        name="second_attend",
    )(core, own, other, *tabs)


def exchange(x, axes):
    return lax.all_to_all(x, axes, split_axis=0, concat_axis=0, tiled=True)


def swap(x):
    return lax.ppermute(x, "core", [(0, 1), (1, 0)])


def document_begins(note):
    group = lax.axis_index("dp")
    units = lax.dynamic_slice(note, (COLS * group, 0, PER), (COLS, 2, 2)).reshape(16)
    return jnp.sum((units[None, :] < units[:, None]).astype(jnp.int32), axis=1)


def per_device(queries, keys, values, plan, segment_ids):
    core = lax.axis_index("core").astype(jnp.int32)
    cores = core.reshape(1)
    send_0, perm, back = first_pack(plan, segment_ids, keys, values, queries)
    send_1 = second_pack(cores, perm, queries)
    got_0 = exchange(send_0, FLAT)
    got_0, send_1 = lax.optimization_barrier((got_0, send_1))
    got_0 = got_0.reshape(CHIPS, 2, -1, HD)
    own_1 = exchange(send_1, CHIP_AXES)
    note = got_0[:, :, got_0.shape[2] - NOTE].astype(f32)
    sides = jnp.where(core == 0, note, note[:, ::-1])
    sides = jnp.concatenate([sides[:, 0], sides[:, 1]], axis=0)
    out_0, tabs = first_attend(cores, document_begins(note), sides, got_0)
    own_1, out_0 = lax.optimization_barrier((own_1, out_0))
    other_1 = swap(own_1)
    home_0 = exchange(out_0, CHIP_AXES)
    out_1 = second_attend(cores, own_1, other_1, tabs)
    home_0, out_1 = lax.optimization_barrier((home_0, out_1))
    home_1 = exchange(out_1.reshape(DEVICES, PART, PER, HD), FLAT)
    result = unpack(cores, back, [home_0, swap(home_0)], 0, None)
    home_1, result = lax.optimization_barrier((home_1, result))
    return unpack(jnp.zeros_like(cores), back, [home_1, home_1], 1, result)


def solution(mesh):
    chips = Mesh(mesh.devices.reshape(GROUPS, COLS, 2), FLAT)
    return jax.shard_map(
        per_device,
        mesh=chips,
        in_specs=(
            P(FLAT, None),
            P(FLAT, None),
            P(FLAT, None),
            P(FLAT),
            P(FLAT),
        ),
        out_specs=P(FLAT, None),
        check_vma=False,
    )
```

```python
import functools

import jax
import jax.numpy as jnp
import numpy as np
from jax import lax
from jax.experimental import pallas as pl
from jax.experimental.pallas import tpu as pltpu
from jax.sharding import Mesh
from jax.sharding import PartitionSpec as P

H = 64
KVH = 8
HD = 128
ROWS = 256
SEQ = 8
GROUPS = 16
COLS = SEQ // 2
CHIPS = GROUPS * COLS
DEVICES = 2 * CHIPS
PER = ROWS // GROUPS
GROUP = SEQ * ROWS
PER_KV = H // KVH
CHUNKS = GROUP // ROWS
PART = 4
NOTE = 8
WIDE = PART * HD
BIG = 1e30
theta_base = 500000.0
MIB = 1024 * 1024

FLAT = ("dp", "z", "core")
CHIP_AXES = ("dp", "z")

f32 = jnp.float32
bf16 = jnp.bfloat16


def params(mib):
    return pltpu.CompilerParams(vmem_limit_bytes=mib * MIB)


def dot(a, b):
    return jnp.dot(a, b, preferred_element_type=f32)


def iota(shape, axis):
    return lax.broadcasted_iota(jnp.int32, shape, axis)


def order(plan_ref, ids_ref, perm_ref, back_ref):
    square = (ROWS, ROWS)
    wide = jnp.broadcast_to(plan_ref[...].astype(f32), square)
    tall = wide.T
    rank_row = jnp.sum((tall < wide).astype(f32), axis=0, keepdims=True).astype(jnp.int32)
    rank_col = jnp.sum((wide < tall).astype(f32), axis=1, keepdims=True).astype(jnp.int32)
    hit = rank_row == iota(square, 0)
    perm_ref[...] = hit.astype(bf16)
    back_ref[...] = (rank_col == iota(square, 1)).astype(bf16)
    ordered = jnp.sum(jnp.where(hit, wide, 0.0), axis=1, keepdims=True).astype(jnp.int32)
    place = (ordered & (ROWS - 1)).astype(f32)
    tall_shape = (ROWS, HD)
    laid = jnp.where((iota(tall_shape, 0) & (PER - 1)) == iota(tall_shape, 1), place, 0.0).astype(bf16)
    flat = (GROUPS * NOTE, ROWS)
    pick = ((iota(flat, 0) >> 3) == (iota(flat, 1) >> 4)).astype(bf16)
    lane = iota((GROUPS * NOTE, HD), 1)
    ids = ids_ref[...].astype(f32)
    note = jnp.where(lane == PER, ids[:, :1], dot(pick, laid))
    return jnp.where(lane == PER + 1, ids[:, ROWS - 1 :], note).astype(bf16)


def lanes(start, width):
    return pl.ds(pl.multiple_of(start, HD), width)


def start(copies):
    for copy in copies:
        copy.start()
    return copies


def wait(copies):
    for copy in copies:
        copy.wait()


def first_pack_kernel(
    plan_ref, ids_ref, k_ref, v_ref, q_ref, out_ref, perm_out, back_out,
    plan_in, ids_in, buffer, built, perm_ref, back_ref, sems, more_sems,
):
    early = start([
        pltpu.make_async_copy(plan_ref, plan_in, more_sems.at[0]),
        pltpu.make_async_copy(ids_ref, ids_in, more_sems.at[1]),
    ])
    copies = []
    for slot in range(SEQ):
        places = (
            (k_ref, slot * HD, 0, HD),
            (v_ref, slot * HD, HD, HD),
            (q_ref, slot * PER_KV * HD, 2 * HD, WIDE),
        )
        copies.append(start([
            pltpu.make_async_copy(
                ref.at[:, pl.ds(here, width)], buffer.at[slot, :, pl.ds(there, width)], sems.at[number, slot]
            )
            for number, (ref, here, there, width) in enumerate(places)
        ]))
    wait(early)
    note = order(plan_in, ids_in, perm_ref, back_ref).reshape(GROUPS, NOTE, HD)
    leaving = start([
        pltpu.make_async_copy(perm_ref, perm_out, more_sems.at[2]),
        pltpu.make_async_copy(back_ref, back_out, more_sems.at[3]),
    ])
    length = (PART + 2) * PER
    for z in range(COLS):
        for c in range(2):
            built[2 * z + c, :, length:, :] = note
    for low in range(0, SEQ, 4):
        for slot in range(low, low + 4):
            wait(copies[slot])
        for slot in range(low, low + 4):
            moved = dot(perm_ref[...], buffer[slot]).astype(bf16)
            for j in range(PART + 2):
                built[slot, :, j * PER : j * PER + PER, :] = moved[:, j * HD : j * HD + HD].reshape(GROUPS, PER, HD)
            leaving += start([pltpu.make_async_copy(built.at[slot], out_ref.at[:, slot], sems.at[3, slot])])
    wait(leaving)


def second_pack_kernel(core_ref, perm_ref, q_ref, keep_ref, give_ref, perm_in, buffer, built, sems, more_sems):
    early = start([pltpu.make_async_copy(perm_ref, perm_in, more_sems.at[0])])
    copies = []
    for z in range(COLS):
        for r in range(2):
            head = 2 * z + (r ^ core_ref[0])
            slot = 2 * z + r
            copies += start([
                pltpu.make_async_copy(
                    q_ref.at[:, lanes(head * (PER_KV * HD) + WIDE, WIDE)], buffer.at[slot], sems.at[0, slot]
                )
            ])
    wait(early)
    leaving = []
    for low in range(0, SEQ, 4):
        wait(copies[low : low + 4])
        for slot in range(low, low + 4):
            moved = dot(perm_in[...], buffer[slot]).astype(bf16)
            for j in range(PART):
                built[slot, :, j * PER : j * PER + PER, :] = moved[:, j * HD : j * HD + HD].reshape(GROUPS, PER, HD)
            z, r = divmod(slot, 2)
            there = keep_ref.at[:, z, 0] if r == 0 else give_ref.at[:, z]
            leaving += start([pltpu.make_async_copy(built.at[slot], there, sems.at[1, slot])])
    wait(leaving)


def lanes(first, width):
    return pl.ds(pl.multiple_of(first, HD), width)


def anywhere():
    return pl.BlockSpec(memory_space=pl.ANY)


def smem():
    return pl.BlockSpec(memory_space=pltpu.SMEM)


def vmem():
    return pl.BlockSpec(memory_space=pltpu.VMEM)


def work(flops, moved, transcendentals=0):
    return pl.CostEstimate(flops=flops, bytes_accessed=moved, transcendentals=transcendentals)


def first_pack(plan, segment_ids, keys, values, queries):
    length = (PART + 2) * PER + NOTE
    square = (ROWS, ROWS)
    out, perm, back = pl.pallas_call(
        first_pack_kernel,
        in_specs=[anywhere()] * 5,
        out_specs=[anywhere()] * 3,
        out_shape=(
            jax.ShapeDtypeStruct((GROUPS, SEQ, length, HD), bf16),
            jax.ShapeDtypeStruct(square, bf16),
            jax.ShapeDtypeStruct(square, bf16),
        ),
        scratch_shapes=[
            pltpu.VMEM((1, ROWS), jnp.int32),
            pltpu.VMEM((1, ROWS), jnp.int32),
            pltpu.VMEM((SEQ, ROWS, (PART + 2) * HD), bf16),
            pltpu.VMEM((SEQ, GROUPS, length, HD), bf16),
            pltpu.VMEM(square, bf16),
            pltpu.VMEM(square, bf16),
            pltpu.SemaphoreType.DMA((4, SEQ)),
            pltpu.SemaphoreType.DMA((4,)),
        ],
        compiler_params=params(60),
        cost_estimate=work(2 * ROWS * ROWS * SEQ * 768, 4 * ROWS * SEQ * 768),
        name="first_pack",
    )(plan.reshape(1, ROWS), segment_ids.reshape(1, ROWS), keys, values, queries)
    return out.reshape(DEVICES, length, HD), perm, back


def second_pack(core, perm, queries):
    length = PART * PER
    keep, give = pl.pallas_call(
        second_pack_kernel,
        in_specs=[smem(), anywhere(), anywhere()],
        out_specs=[anywhere()] * 2,
        out_shape=[
            jax.ShapeDtypeStruct((GROUPS, COLS, 2, length, HD), bf16),
            jax.ShapeDtypeStruct((GROUPS, COLS, length, HD), bf16),
        ],
        scratch_shapes=[
            pltpu.VMEM((ROWS, ROWS), bf16),
            pltpu.VMEM((SEQ, ROWS, WIDE), bf16),
            pltpu.VMEM((SEQ, GROUPS, PART * PER, HD), bf16),
            pltpu.SemaphoreType.DMA((2, SEQ)),
            pltpu.SemaphoreType.DMA((1,)),
        ],
        compiler_params=params(60),
        cost_estimate=work(2 * ROWS * ROWS * SEQ * WIDE, 4 * ROWS * SEQ * WIDE),
        name="second_pack",
    )(core, perm, queries)
    return keep.reshape(CHIPS, 2, length, HD), give.reshape(CHIPS, length, HD)


def place_kernel(taken_ref, keep_ref, out_ref, buffer, sems):
    step = CHIPS // 4
    arriving, leaving = [], []
    for i in range(4):
        here = pl.ds(i * step, step)
        arriving += start([pltpu.make_async_copy(taken_ref.at[here], buffer.at[here], sems.at[0, i])])
        leaving.append(pltpu.make_async_copy(buffer.at[here], out_ref.at[here, 1], sems.at[1, i]))
    for coming, going in zip(arriving, leaving):
        coming.wait()
        going.start()
    wait(leaving)


def place(keep, taken):
    return pl.pallas_call(
        place_kernel,
        in_specs=[anywhere()] * 2,
        out_specs=anywhere(),
        out_shape=jax.ShapeDtypeStruct(keep.shape, keep.dtype),
        scratch_shapes=[pltpu.VMEM(taken.shape, taken.dtype), pltpu.SemaphoreType.DMA((2, 4))],
        input_output_aliases={1: 0},
        compiler_params=params(16),
        cost_estimate=work(0, 2 * taken.size * 2),
        name="place",
    )(taken, keep)


def unpack_kernel(part, core_ref, back_ref, *refs):
    sources = refs[:2]
    out_ref, back_in, buffer, built, sems, more_sems = refs[-6:]
    early = start([pltpu.make_async_copy(back_ref, back_in, more_sems.at[0])])
    arriving, leaving = [], []
    for r in range(2):
        for z in range(COLS):
            slot = r * COLS + z
            arriving += start([pltpu.make_async_copy(sources[r].at[:, z, r], buffer.at[slot], sems.at[0, slot])])
    wait(early)
    for r in range(2):
        wait(arriving[r * COLS : r * COLS + COLS])
        for z in range(COLS):
            slot = r * COLS + z
            heads = [buffer[slot, :, j].reshape(ROWS, HD) for j in range(PART)]
            built[slot] = dot(back_in[...], jnp.concatenate(heads, axis=1)).astype(bf16)
            here = lanes((2 * z + (r ^ core_ref[0])) * (PER_KV * HD) + part * WIDE, WIDE)
            leaving += start([pltpu.make_async_copy(built.at[slot], out_ref.at[:, here], sems.at[1, slot])])
    wait(leaving)


def unpack(core, back, homes, part, into):
    more = [] if into is None else [into]
    return pl.pallas_call(
        functools.partial(unpack_kernel, part),
        in_specs=[smem()] + [anywhere()] * (3 + len(more)),
        out_specs=anywhere(),
        out_shape=jax.ShapeDtypeStruct((ROWS, H * HD), bf16),
        scratch_shapes=[
            pltpu.VMEM((ROWS, ROWS), bf16),
            pltpu.VMEM((SEQ, GROUPS, PART, PER, HD), bf16),
            pltpu.VMEM((SEQ, ROWS, WIDE), bf16),
            pltpu.SemaphoreType.DMA((2, SEQ)),
            pltpu.SemaphoreType.DMA((1,)),
        ],
        input_output_aliases={} if into is None else {4: 0},
        compiler_params=params(16),
        cost_estimate=work(2 * ROWS * ROWS * SEQ * WIDE, 4 * ROWS * SEQ * WIDE),
        name="unpack_rows",
    )(core, back, *[home.reshape(GROUPS, COLS, 2, PART, PER, HD) for home in homes], *more)


def turn_table():
    freqs = np.float32(theta_base) ** (np.float32(-2.0) * np.arange(HD // 2, dtype=np.float32) / np.float32(HD))
    freqs = freqs.astype(np.float64)
    low = np.arange(HD, dtype=np.float64)[:, None] * freqs[None, :]
    table = np.concatenate([np.cos(low), np.sin(low)], axis=1)
    terms = []
    for _ in range(3):
        term = table.astype(jnp.bfloat16)
        terms.append(term)
        table = table - term.astype(np.float64)
    high = 128.0 * np.arange(16, dtype=np.float64)[:, None] * freqs[None, :]
    c, s = np.cos(high), np.sin(high)
    tops = np.stack([np.concatenate(pair, axis=1) for pair in ((c, -s), (-s, c), (-c, s))])
    return np.concatenate(terms, axis=1), tops.astype(np.float32)


def source(j):
    return ((j >> 1) & 15) * 16 + 2 * (j >> 5) + (j & 1)


def chunk_of(x_ref, chunk, number):
    side = chunk // (CHUNKS // 2)
    loaders = pl.ds(chunk % (CHUNKS // 2) * 16, 16)
    return x_ref[side, loaders, number * PER : number * PER + PER].reshape(ROWS, HD)


def chunk_rows(chunk, s):
    return pl.ds(s * ROWS + chunk * 32, 32)


def settle():
    square = (ROWS, ROWS)
    return (source(iota(square, 0)) == iota(square, 1)).astype(bf16)


def unsettle():
    square = (ROWS, ROWS)
    return (source(iota(square, 1)) == iota(square, 0)).astype(bf16)


def prepare(begin_ref, x_ref, note_ref, low_ref, tops_ref, tabs, place_ref):
    turn_c_ref, turn_s_ref, q_mark_ref, kt_ref, vv_ref, causal_ref = tabs
    perm = settle()
    strip = (ROWS, 16)
    loader = (((iota(strip, 0) >> 1) & 15) == iota(strip, 1)).astype(bf16)
    wide = (ROWS, HD)
    row, lane = iota(wide, 0), iota(wide, 1)
    slot = lane == 2 * (row >> 5) + (row & 1)
    ones = jnp.ones((HD, HD), bf16)
    lane = iota((32, HD), 1)
    for chunk in range(CHUNKS):
        notes = note_ref[pl.ds(chunk * 16, 16), :]
        spread = dot(loader, notes.astype(bf16))
        place = dot(jnp.where(slot, spread, 0.0).astype(bf16), ones)
        low = (place.astype(jnp.int32) & (HD - 1)) == iota(wide, 1)
        parts = dot(low.astype(bf16), low_ref[...])
        here = parts[:, :HD] + (parts[:, HD : 2 * HD] + parts[:, 2 * HD :])
        swapped = pltpu.roll(here, HD // 2, 1)
        both = dot(perm, jnp.concatenate([chunk_of(x_ref, chunk, 0), chunk_of(x_ref, chunk, 1)], axis=1))
        keys, values = both[:, :HD], both[:, HD:].astype(bf16)
        keys_swapped = pltpu.roll(keys, HD // 2, 1)
        for s in range(SEQ):
            piece = slice(s * 32, s * 32 + 32)
            at = chunk_rows(chunk, s)
            same = pl.ds(chunk * ROWS + s * 32, 32)
            mine = place[piece, :]
            place_ref[at, :] = mine
            first = mine < float(HD)
            begins = begin_ref[2 * s], begin_ref[2 * s + 1]
            gaps = 2 * s - begins[0], 2 * s + 1 - begins[1]
            top = [jnp.where(first, tops_ref[i, pl.ds(gaps[0], 1), :], tops_ref[i, pl.ds(gaps[1], 1), :]) for i in range(3)]
            turn_c = here[piece, :] * top[0] + swapped[piece, :] * top[1]
            turn_s = here[piece, :] * top[1] + swapped[piece, :] * top[2]
            turn_c_ref[same, :] = turn_c
            turn_s_ref[same, :] = turn_s
            q_mark_ref[at, :] = jnp.where(lane < jnp.where(first, begins[0], begins[1]), -BIG, 0.0).astype(bf16)
            turned = keys[piece, :] * turn_c + keys_swapped[piece, :] * turn_s
            vv_ref[at, HD:] = turned.astype(bf16)
            vv_ref[at, :HD] = values[piece, :]

    for s in range(SEQ):
        at = slice(s * ROWS, s * ROWS + ROWS)
        kt_ref[:HD, at] = vv_ref[at, HD:].astype(f32).T.astype(bf16)
        across = place_ref[at, :].T
        unit = jnp.where(across < float(HD), 2 * s, 2 * s + 1)
        kt_ref[HD:, at] = (unit == iota((HD, ROWS), 0)).astype(bf16)
        down = jnp.concatenate([place_ref[at, :], place_ref[at, :]], axis=1)
        causal_ref[at, :] = jnp.where(across[:1, :] <= down, 0.0, -BIG)
    vv_ref[:, HD:] = jnp.ones((GROUP, HD), bf16)


def take_queries(x_ref, first, tabs, qs_ref):
    turn_c_ref, turn_s_ref, q_mark_ref = tabs[:3]
    perm = settle()
    for chunk in range(CHUNKS):
        moved = dot(perm, jnp.concatenate([chunk_of(x_ref, chunk, first + h) for h in range(PART)], axis=1))
        same = pl.ds(chunk * ROWS, ROWS)
        turn_c, turn_s = turn_c_ref[same, :], turn_s_ref[same, :]
        for h in range(PART):
            one = moved[:, h * HD : h * HD + HD]
            one = (one * turn_c + pltpu.roll(one, HD // 2, 1) * turn_s).astype(bf16)
            for s in range(SEQ):
                qs_ref[s, chunk_rows(chunk, h), :HD] = one[s * 32 : s * 32 + 32]

    for s in range(SEQ):
        for h in range(PART):
            qs_ref[s, h * ROWS : h * ROWS + ROWS, HD:] = q_mark_ref[s * ROWS : s * ROWS + ROWS, :]


def attend_blocks(tabs, qs_ref, os_ref):
    kt_ref, vv_ref, causal_ref = tabs[3:]
    factor = (HD ** -0.5) * 1.4426950408889634

    def scores(s, rows):
        return dot(qs_ref[s, rows, :], kt_ref[:, : s * ROWS + ROWS])

    def finish(s, rows, score):
        here = slice(s * ROWS, s * ROWS + ROWS)
        diagonal = score[:, s * ROWS :] + causal_ref[here, :]
        score = diagonal if s == 0 else jnp.concatenate([score[:, : s * ROWS], diagonal], axis=1)
        peak = jnp.max(score, axis=1, keepdims=True)
        weight = jnp.exp2((score - peak) * factor).astype(bf16)
        mixed = dot(weight, vv_ref[: s * ROWS + ROWS, :])
        os_ref[s, rows, :] = (mixed[:, :HD] / mixed[:, HD:]).astype(bf16)

    @pl.loop(0, PART // 2)
    def _(pair):
        rows = [pl.ds(pl.multiple_of((2 * pair + i) * ROWS, ROWS), ROWS) for i in range(2)]
        items = [(s, rows[i]) for s in range(SEQ) for i in range(2)]
        score = scores(*items[0])
        for number, item in enumerate(items):
            following = scores(*items[number + 1]) if number + 1 < len(items) else None
            finish(*item, score)
            score = following


def give_back(os_ref, built, targets, sems):
    perm = unsettle()

    def going(side, at):
        chunk = side * (CHUNKS // 2) + at
        there = targets[side].at[pl.ds(at * 16, 16)]
        return pltpu.make_async_copy(built.at[chunk], there, sems.at[chunk])

    for side in range(2):
        for at in range(CHUNKS // 2):
            chunk = side * (CHUNKS // 2) + at
            heads = []
            for h in range(PART):
                heads.append(jnp.concatenate([os_ref[s, chunk_rows(chunk, h), :] for s in range(SEQ)], axis=0))
            moved = dot(perm, jnp.concatenate(heads, axis=1)).astype(bf16)
            for h in range(PART):
                built[chunk, :, h] = moved[:, h * HD : h * HD + HD].reshape(16, PER, HD)
            going(side, at).start()

    return [going(side, at) for side in range(2) for at in range(CHUNKS // 2)]


def attend_kernel(
    second, core_ref, begin_ref, note_ref, low_ref, tops_ref, kv_ref, q_ref, out_ref,
    kv_in, q_in, place_ref, qs_ref, os_ref, built, turn_c, turn_s, q_mark, kt, vv, causal, sems, out_sems,
):
    tabs = turn_c, turn_s, q_mark, kt, vv, causal
    core = core_ref[0]
    arriving = []
    for side in range(2):
        here = kv_ref.at[:, side ^ core, : 2 * PER]
        arriving += start([pltpu.make_async_copy(here, kv_in.at[side], sems.at[0, side])])
    for side in range(2):
        here = q_ref.at[:, side] if second else q_ref.at[:, side ^ core, 2 * PER : (2 + PART) * PER]
        arriving += start([pltpu.make_async_copy(here, q_in.at[side], sems.at[1, side])])
    wait(arriving[:2])
    prepare(begin_ref, kv_in, note_ref, low_ref, tops_ref, tabs, place_ref)
    wait(arriving[2:])
    take_queries(q_in, 0, tabs, qs_ref)
    attend_blocks(tabs, qs_ref, os_ref)
    targets = [out_ref.at[:, side ^ core] if second else out_ref.at[:, side] for side in range(2)]
    wait(give_back(os_ref, built, targets, out_sems))


def attend(second, core, begin, note, kv, queries):
    low, tops = turn_table()
    pairs = PART * GROUP * GROUP * 36 // 64
    return pl.pallas_call(
        functools.partial(attend_kernel, second),
        in_specs=[smem(), smem(), vmem(), vmem(), vmem(), anywhere(), anywhere()],
        out_specs=anywhere(),
        out_shape=jax.ShapeDtypeStruct((CHIPS, 2, PART, PER, HD), bf16),
        scratch_shapes=[
            pltpu.VMEM((2, CHIPS, 2 * PER, HD), bf16),
            pltpu.VMEM((2, CHIPS, PART * PER, HD), bf16),
            pltpu.VMEM((GROUP, HD), f32),
            pltpu.VMEM((SEQ, PART * ROWS, 2 * HD), bf16),
            pltpu.VMEM((SEQ, PART * ROWS, HD), bf16),
            pltpu.VMEM((CHUNKS, 16, PART, PER, HD), bf16),
            pltpu.VMEM((GROUP, HD), f32),
            pltpu.VMEM((GROUP, HD), f32),
            pltpu.VMEM((GROUP, HD), bf16),
            pltpu.VMEM((2 * HD, GROUP), bf16),
            pltpu.VMEM((GROUP, 2 * HD), bf16),
            pltpu.VMEM((GROUP, ROWS), f32),
            pltpu.SemaphoreType.DMA((2, 2)),
            pltpu.SemaphoreType.DMA((CHUNKS,)),
        ],
        compiler_params=params(60),
        cost_estimate=work(pairs * 4 * 256, 16 * MIB, pairs),
        name="attend",
    )(core, begin, note, jnp.asarray(low), jnp.asarray(tops), kv, queries)


def exchange(x, axes):
    return lax.all_to_all(x, axes, split_axis=0, concat_axis=0, tiled=True)


def swap(x):
    return lax.ppermute(x, "core", [(0, 1), (1, 0)])


def document_begins(note):
    group = lax.axis_index("dp")
    units = lax.dynamic_slice(note, (COLS * group, 0, PER), (COLS, 2, 2)).reshape(16)
    return jnp.sum((units[None, :] < units[:, None]).astype(jnp.int32), axis=1)


def per_device(queries, keys, values, plan, segment_ids):
    core = lax.axis_index("core").astype(jnp.int32)
    cores = core.reshape(1)
    send_0, perm, back = first_pack(plan, segment_ids, keys, values, queries)
    keep, give = second_pack(cores, perm, queries)
    send_1 = place(keep, swap(give))
    got_0 = exchange(send_0, FLAT)
    got_0, send_1 = lax.optimization_barrier((got_0, send_1))
    got_0 = got_0.reshape(CHIPS, 2, -1, HD)
    got_1 = exchange(send_1, CHIP_AXES)
    note = got_0[:, :, got_0.shape[2] - NOTE].astype(f32)
    sides = jnp.where(core == 0, note, note[:, ::-1])
    sides = jnp.concatenate([sides[:, 0], sides[:, 1]], axis=0)
    begin = document_begins(note)
    out_0 = attend(False, cores, begin, sides, got_0, got_0)
    got_1, out_0 = lax.optimization_barrier((got_1, out_0))
    home_0 = exchange(out_0, CHIP_AXES)
    out_1 = attend(True, cores, begin, sides, got_0, got_1)
    home_0, out_1 = lax.optimization_barrier((home_0, out_1))
    home_1 = exchange(out_1.reshape(DEVICES, PART, PER, HD), FLAT)
    result = unpack(cores, back, [home_0, swap(home_0)], 0, None)
    home_1, result = lax.optimization_barrier((home_1, result))
    return unpack(jnp.zeros_like(cores), back, [home_1, home_1], 1, result)


def solution(mesh):
    chips = Mesh(mesh.devices.reshape(GROUPS, COLS, 2), FLAT)
    return jax.shard_map(
        per_device,
        mesh=chips,
        in_specs=(
            P(FLAT, None),
            P(FLAT, None),
            P(FLAT, None),
            P(FLAT),
            P(FLAT),
        ),
        out_specs=P(FLAT, None),
        check_vma=False,
    )
```

```python
import functools

import jax
import jax.numpy as jnp
import numpy as np
from jax import lax
from jax.experimental import pallas as pl
from jax.experimental.pallas import tpu as pltpu
from jax.sharding import Mesh
from jax.sharding import PartitionSpec as P

H = 64
KVH = 8
HD = 128
ROWS = 256
SEQ = 8
GROUPS = 16
COLS = SEQ // 2
CHIPS = GROUPS * COLS
DEVICES = 2 * CHIPS
PER = ROWS // GROUPS
GROUP = SEQ * ROWS
PER_KV = H // KVH
CHUNKS = GROUP // ROWS
PART = 4
NOTE = 8
WIDE = PART * HD
BIG = 1e30
theta_base = 500000.0
MIB = 1024 * 1024

FLAT = ("dp", "z", "core")
CHIP_AXES = ("dp", "z")

f32 = jnp.float32
bf16 = jnp.bfloat16


def params(mib):
    return pltpu.CompilerParams(vmem_limit_bytes=mib * MIB)


def dot(a, b):
    return jnp.dot(a, b, preferred_element_type=f32)


def iota(shape, axis):
    return lax.broadcasted_iota(jnp.int32, shape, axis)


def order(plan_ref, ids_ref, perm_ref, back_ref):
    square = (ROWS, ROWS)
    wide = jnp.broadcast_to(plan_ref[...].astype(f32), square)
    tall = wide.T
    rank_row = jnp.sum((tall < wide).astype(f32), axis=0, keepdims=True).astype(jnp.int32)
    rank_col = jnp.sum((wide < tall).astype(f32), axis=1, keepdims=True).astype(jnp.int32)
    hit = rank_row == iota(square, 0)
    perm_ref[...] = hit.astype(bf16)
    back_ref[...] = (rank_col == iota(square, 1)).astype(bf16)
    ordered = jnp.sum(jnp.where(hit, wide, 0.0), axis=1, keepdims=True).astype(jnp.int32)
    place = (ordered & (ROWS - 1)).astype(f32)
    tall_shape = (ROWS, HD)
    laid = jnp.where((iota(tall_shape, 0) & (PER - 1)) == iota(tall_shape, 1), place, 0.0).astype(bf16)
    flat = (GROUPS * NOTE, ROWS)
    pick = ((iota(flat, 0) >> 3) == (iota(flat, 1) >> 4)).astype(bf16)
    lane = iota((GROUPS * NOTE, HD), 1)
    ids = ids_ref[...].astype(f32)
    note = jnp.where(lane == PER, ids[:, :1], dot(pick, laid))
    return jnp.where(lane == PER + 1, ids[:, ROWS - 1 :], note).astype(bf16)


def lanes(start, width):
    return pl.ds(pl.multiple_of(start, HD), width)


def start(copies):
    for copy in copies:
        copy.start()
    return copies


def wait(copies):
    for copy in copies:
        copy.wait()


def first_pack_kernel(
    plan_ref, ids_ref, k_ref, v_ref, q_ref, out_ref, perm_out, back_out,
    plan_in, ids_in, buffer, built, perm_ref, back_ref, sems, more_sems,
):
    early = start([
        pltpu.make_async_copy(plan_ref, plan_in, more_sems.at[0]),
        pltpu.make_async_copy(ids_ref, ids_in, more_sems.at[1]),
    ])
    copies = []
    for slot in range(SEQ):
        places = (
            (k_ref, slot * HD, 0, HD),
            (v_ref, slot * HD, HD, HD),
            (q_ref, slot * PER_KV * HD, 2 * HD, WIDE),
        )
        copies.append(start([
            pltpu.make_async_copy(
                ref.at[:, pl.ds(here, width)], buffer.at[slot, :, pl.ds(there, width)], sems.at[number, slot]
            )
            for number, (ref, here, there, width) in enumerate(places)
        ]))
    wait(early)
    note = order(plan_in, ids_in, perm_ref, back_ref).reshape(GROUPS, NOTE, HD)
    leaving = start([
        pltpu.make_async_copy(perm_ref, perm_out, more_sems.at[2]),
        pltpu.make_async_copy(back_ref, back_out, more_sems.at[3]),
    ])
    length = (PART + 2) * PER
    for z in range(COLS):
        for c in range(2):
            built[2 * z + c, :, length:, :] = note
    for low in range(0, SEQ, 4):
        for slot in range(low, low + 4):
            wait(copies[slot])
        for slot in range(low, low + 4):
            moved = dot(perm_ref[...], buffer[slot]).astype(bf16)
            for j in range(PART + 2):
                built[slot, :, j * PER : j * PER + PER, :] = moved[:, j * HD : j * HD + HD].reshape(GROUPS, PER, HD)
            leaving += start([pltpu.make_async_copy(built.at[slot], out_ref.at[:, slot], sems.at[3, slot])])
    wait(leaving)


def second_pack_kernel(core_ref, perm_ref, q_ref, keep_ref, give_ref, perm_in, buffer, built, sems, more_sems):
    early = start([pltpu.make_async_copy(perm_ref, perm_in, more_sems.at[0])])
    copies = []
    for z in range(COLS):
        for r in range(2):
            head = 2 * z + (r ^ core_ref[0])
            slot = 2 * z + r
            copies += start([
                pltpu.make_async_copy(
                    q_ref.at[:, lanes(head * (PER_KV * HD) + WIDE, WIDE)], buffer.at[slot], sems.at[0, slot]
                )
            ])
    wait(early)
    leaving = []
    for low in range(0, SEQ, 4):
        wait(copies[low : low + 4])
        for slot in range(low, low + 4):
            moved = dot(perm_in[...], buffer[slot]).astype(bf16)
            for j in range(PART):
                built[slot, :, j * PER : j * PER + PER, :] = moved[:, j * HD : j * HD + HD].reshape(GROUPS, PER, HD)
            z, r = divmod(slot, 2)
            there = keep_ref.at[:, z, 0] if r == 0 else give_ref.at[:, z]
            leaving += start([pltpu.make_async_copy(built.at[slot], there, sems.at[1, slot])])
    wait(leaving)


def lanes(first, width):
    return pl.ds(pl.multiple_of(first, HD), width)


def anywhere():
    return pl.BlockSpec(memory_space=pl.ANY)


def smem():
    return pl.BlockSpec(memory_space=pltpu.SMEM)


def vmem():
    return pl.BlockSpec(memory_space=pltpu.VMEM)


def work(flops, moved, transcendentals=0):
    return pl.CostEstimate(flops=flops, bytes_accessed=moved, transcendentals=transcendentals)


def first_pack(plan, segment_ids, keys, values, queries):
    length = (PART + 2) * PER + NOTE
    square = (ROWS, ROWS)
    out, perm, back = pl.pallas_call(
        first_pack_kernel,
        in_specs=[anywhere()] * 5,
        out_specs=[anywhere()] * 3,
        out_shape=(
            jax.ShapeDtypeStruct((GROUPS, SEQ, length, HD), bf16),
            jax.ShapeDtypeStruct(square, bf16),
            jax.ShapeDtypeStruct(square, bf16),
        ),
        scratch_shapes=[
            pltpu.VMEM((1, ROWS), jnp.int32),
            pltpu.VMEM((1, ROWS), jnp.int32),
            pltpu.VMEM((SEQ, ROWS, (PART + 2) * HD), bf16),
            pltpu.VMEM((SEQ, GROUPS, length, HD), bf16),
            pltpu.VMEM(square, bf16),
            pltpu.VMEM(square, bf16),
            pltpu.SemaphoreType.DMA((4, SEQ)),
            pltpu.SemaphoreType.DMA((4,)),
        ],
        compiler_params=params(60),
        cost_estimate=work(2 * ROWS * ROWS * SEQ * 768, 4 * ROWS * SEQ * 768),
        name="first_pack",
    )(plan.reshape(1, ROWS), segment_ids.reshape(1, ROWS), keys, values, queries)
    return out.reshape(DEVICES, length, HD), perm, back


def second_pack(core, perm, queries):
    length = PART * PER
    keep, give = pl.pallas_call(
        second_pack_kernel,
        in_specs=[smem(), anywhere(), anywhere()],
        out_specs=[anywhere()] * 2,
        out_shape=[
            jax.ShapeDtypeStruct((GROUPS, COLS, 2, length, HD), bf16),
            jax.ShapeDtypeStruct((GROUPS, COLS, length, HD), bf16),
        ],
        scratch_shapes=[
            pltpu.VMEM((ROWS, ROWS), bf16),
            pltpu.VMEM((SEQ, ROWS, WIDE), bf16),
            pltpu.VMEM((SEQ, GROUPS, PART * PER, HD), bf16),
            pltpu.SemaphoreType.DMA((2, SEQ)),
            pltpu.SemaphoreType.DMA((1,)),
        ],
        compiler_params=params(60),
        cost_estimate=work(2 * ROWS * ROWS * SEQ * WIDE, 4 * ROWS * SEQ * WIDE),
        name="second_pack",
    )(core, perm, queries)
    return keep.reshape(CHIPS, 2, length, HD), give.reshape(CHIPS, length, HD)


def place_kernel(taken_ref, keep_ref, out_ref, buffer, sems):
    step = CHIPS // 4
    arriving, leaving = [], []
    for i in range(4):
        here = pl.ds(i * step, step)
        arriving += start([pltpu.make_async_copy(taken_ref.at[here], buffer.at[here], sems.at[0, i])])
        leaving.append(pltpu.make_async_copy(buffer.at[here], out_ref.at[here, 1], sems.at[1, i]))
    for coming, going in zip(arriving, leaving):
        coming.wait()
        going.start()
    wait(leaving)


def place(keep, taken):
    return pl.pallas_call(
        place_kernel,
        in_specs=[anywhere()] * 2,
        out_specs=anywhere(),
        out_shape=jax.ShapeDtypeStruct(keep.shape, keep.dtype),
        scratch_shapes=[pltpu.VMEM(taken.shape, taken.dtype), pltpu.SemaphoreType.DMA((2, 4))],
        input_output_aliases={1: 0},
        compiler_params=params(16),
        cost_estimate=work(0, 2 * taken.size * 2),
        name="place",
    )(taken, keep)


def unpack_kernel(part, core_ref, back_ref, *refs):
    sources = refs[:2]
    out_ref, back_in, buffer, built, sems, more_sems = refs[-6:]
    early = start([pltpu.make_async_copy(back_ref, back_in, more_sems.at[0])])
    arriving, leaving = [], []
    for r in range(2):
        for z in range(COLS):
            slot = r * COLS + z
            here = sources[r].at[:, z, r] if len(sources[r].shape) == 6 else sources[r].at[:, z]
            arriving += start([pltpu.make_async_copy(here, buffer.at[slot], sems.at[0, slot])])
    wait(early)
    for r in range(2):
        wait(arriving[r * COLS : r * COLS + COLS])
        for z in range(COLS):
            slot = r * COLS + z
            heads = [buffer[slot, :, j].reshape(ROWS, HD) for j in range(PART)]
            built[slot] = dot(back_in[...], jnp.concatenate(heads, axis=1)).astype(bf16)
            here = lanes((2 * z + (r ^ core_ref[0])) * (PER_KV * HD) + part * WIDE, WIDE)
            leaving += start([pltpu.make_async_copy(built.at[slot], out_ref.at[:, here], sems.at[1, slot])])
    wait(leaving)


def unpack(core, back, homes, part, into):
    more = [] if into is None else [into]
    return pl.pallas_call(
        functools.partial(unpack_kernel, part),
        in_specs=[smem()] + [anywhere()] * (3 + len(more)),
        out_specs=anywhere(),
        out_shape=jax.ShapeDtypeStruct((ROWS, H * HD), bf16),
        scratch_shapes=[
            pltpu.VMEM((ROWS, ROWS), bf16),
            pltpu.VMEM((SEQ, GROUPS, PART, PER, HD), bf16),
            pltpu.VMEM((SEQ, ROWS, WIDE), bf16),
            pltpu.SemaphoreType.DMA((2, SEQ)),
            pltpu.SemaphoreType.DMA((1,)),
        ],
        input_output_aliases={} if into is None else {4: 0},
        compiler_params=params(16),
        cost_estimate=work(2 * ROWS * ROWS * SEQ * WIDE, 4 * ROWS * SEQ * WIDE),
        name="unpack_rows",
    )(core, back, *[home.reshape(GROUPS, COLS, *home.shape[1:]) for home in homes], *more)


def turn_table():
    freqs = np.float32(theta_base) ** (np.float32(-2.0) * np.arange(HD // 2, dtype=np.float32) / np.float32(HD))
    freqs = freqs.astype(np.float64)
    low = np.arange(HD, dtype=np.float64)[:, None] * freqs[None, :]
    table = np.concatenate([np.cos(low), np.sin(low)], axis=1)
    terms = []
    for _ in range(3):
        term = table.astype(jnp.bfloat16)
        terms.append(term)
        table = table - term.astype(np.float64)
    high = 128.0 * np.arange(16, dtype=np.float64)[:, None] * freqs[None, :]
    c, s = np.cos(high), np.sin(high)
    tops = np.stack([np.concatenate(pair, axis=1) for pair in ((c, -s), (-s, c), (-c, s))])
    return np.concatenate(terms, axis=1), tops.astype(np.float32)


def source(j):
    return ((j >> 1) & 15) * 16 + 2 * (j >> 5) + (j & 1)


def chunk_of(x_ref, chunk, number):
    side = chunk // (CHUNKS // 2)
    loaders = pl.ds(chunk % (CHUNKS // 2) * 16, 16)
    return x_ref[side, loaders, number * PER : number * PER + PER].reshape(ROWS, HD)


def chunk_rows(chunk, s):
    return pl.ds(s * ROWS + chunk * 32, 32)


def settle():
    square = (ROWS, ROWS)
    return (source(iota(square, 0)) == iota(square, 1)).astype(bf16)


def unsettle():
    square = (ROWS, ROWS)
    return (source(iota(square, 1)) == iota(square, 0)).astype(bf16)


def prepare(begin_ref, x_ref, note_ref, low_ref, tops_ref, tabs, place_ref):
    turn_c_ref, turn_s_ref, q_mark_ref, kt_ref, vv_ref, causal_ref = tabs
    perm = settle()
    strip = (ROWS, 16)
    loader = (((iota(strip, 0) >> 1) & 15) == iota(strip, 1)).astype(bf16)
    wide = (ROWS, HD)
    row, lane = iota(wide, 0), iota(wide, 1)
    slot = lane == 2 * (row >> 5) + (row & 1)
    ones = jnp.ones((HD, HD), bf16)
    lane = iota((32, HD), 1)
    for chunk in range(CHUNKS):
        notes = note_ref[pl.ds(chunk * 16, 16), :]
        spread = dot(loader, notes.astype(bf16))
        place = dot(jnp.where(slot, spread, 0.0).astype(bf16), ones)
        low = (place.astype(jnp.int32) & (HD - 1)) == iota(wide, 1)
        parts = dot(low.astype(bf16), low_ref[...])
        here = parts[:, :HD] + (parts[:, HD : 2 * HD] + parts[:, 2 * HD :])
        swapped = pltpu.roll(here, HD // 2, 1)
        both = dot(perm, jnp.concatenate([chunk_of(x_ref, chunk, 0), chunk_of(x_ref, chunk, 1)], axis=1))
        keys, values = both[:, :HD], both[:, HD:].astype(bf16)
        keys_swapped = pltpu.roll(keys, HD // 2, 1)
        for s in range(SEQ):
            piece = slice(s * 32, s * 32 + 32)
            at = chunk_rows(chunk, s)
            same = pl.ds(chunk * ROWS + s * 32, 32)
            mine = place[piece, :]
            place_ref[at, :] = mine
            first = mine < float(HD)
            begins = begin_ref[2 * s], begin_ref[2 * s + 1]
            gaps = 2 * s - begins[0], 2 * s + 1 - begins[1]
            top = [jnp.where(first, tops_ref[i, pl.ds(gaps[0], 1), :], tops_ref[i, pl.ds(gaps[1], 1), :]) for i in range(3)]
            turn_c = here[piece, :] * top[0] + swapped[piece, :] * top[1]
            turn_s = here[piece, :] * top[1] + swapped[piece, :] * top[2]
            turn_c_ref[same, :] = turn_c
            turn_s_ref[same, :] = turn_s
            q_mark_ref[at, :] = jnp.where(lane < jnp.where(first, begins[0], begins[1]), -BIG, 0.0).astype(bf16)
            turned = keys[piece, :] * turn_c + keys_swapped[piece, :] * turn_s
            vv_ref[at, HD:] = turned.astype(bf16)
            vv_ref[at, :HD] = values[piece, :]

    for s in range(SEQ):
        at = slice(s * ROWS, s * ROWS + ROWS)
        kt_ref[:HD, at] = vv_ref[at, HD:].astype(f32).T.astype(bf16)
        across = place_ref[at, :].T
        unit = jnp.where(across < float(HD), 2 * s, 2 * s + 1)
        kt_ref[HD:, at] = (unit == iota((HD, ROWS), 0)).astype(bf16)
        down = jnp.concatenate([place_ref[at, :], place_ref[at, :]], axis=1)
        causal_ref[at, :] = jnp.where(across[:1, :] <= down, 0.0, -BIG)
    vv_ref[:, HD:] = jnp.ones((GROUP, HD), bf16)


def take_queries(x_ref, first, tabs, qs_ref):
    turn_c_ref, turn_s_ref, q_mark_ref = tabs[:3]
    perm = settle()
    for chunk in range(CHUNKS):
        moved = dot(perm, jnp.concatenate([chunk_of(x_ref, chunk, first + h) for h in range(PART)], axis=1))
        same = pl.ds(chunk * ROWS, ROWS)
        turn_c, turn_s = turn_c_ref[same, :], turn_s_ref[same, :]
        for h in range(PART):
            one = moved[:, h * HD : h * HD + HD]
            one = (one * turn_c + pltpu.roll(one, HD // 2, 1) * turn_s).astype(bf16)
            for s in range(SEQ):
                qs_ref[s, chunk_rows(chunk, h), :HD] = one[s * 32 : s * 32 + 32]

    for s in range(SEQ):
        for h in range(PART):
            qs_ref[s, h * ROWS : h * ROWS + ROWS, HD:] = q_mark_ref[s * ROWS : s * ROWS + ROWS, :]


def attend_blocks(tabs, qs_ref, os_ref):
    kt_ref, vv_ref, causal_ref = tabs[3:]
    factor = (HD ** -0.5) * 1.4426950408889634

    def scores(s, rows):
        return dot(qs_ref[s, rows, :], kt_ref[:, : s * ROWS + ROWS])

    def finish(s, rows, score):
        here = slice(s * ROWS, s * ROWS + ROWS)
        diagonal = score[:, s * ROWS :] + causal_ref[here, :]
        score = diagonal if s == 0 else jnp.concatenate([score[:, : s * ROWS], diagonal], axis=1)
        peak = jnp.max(score, axis=1, keepdims=True)
        weight = jnp.exp2((score - peak) * factor).astype(bf16)
        mixed = dot(weight, vv_ref[: s * ROWS + ROWS, :])
        os_ref[s, rows, :] = (mixed[:, :HD] / mixed[:, HD:]).astype(bf16)

    @pl.loop(0, PART // 2)
    def _(pair):
        rows = [pl.ds(pl.multiple_of((2 * pair + i) * ROWS, ROWS), ROWS) for i in range(2)]
        items = [(s, rows[i]) for s in range(SEQ) for i in range(2)]
        score = scores(*items[0])
        for number, item in enumerate(items):
            following = scores(*items[number + 1]) if number + 1 < len(items) else None
            finish(*item, score)
            score = following


def give_back(os_ref, built, targets, sems):
    perm = unsettle()

    def going(side, at):
        chunk = side * (CHUNKS // 2) + at
        there = targets[side].at[pl.ds(at * 16, 16)]
        return pltpu.make_async_copy(built.at[chunk], there, sems.at[chunk])

    for side in range(2):
        for at in range(CHUNKS // 2):
            chunk = side * (CHUNKS // 2) + at
            heads = []
            for h in range(PART):
                heads.append(jnp.concatenate([os_ref[s, chunk_rows(chunk, h), :] for s in range(SEQ)], axis=0))
            moved = dot(perm, jnp.concatenate(heads, axis=1)).astype(bf16)
            for h in range(PART):
                built[chunk, :, h] = moved[:, h * HD : h * HD + HD].reshape(16, PER, HD)
            going(side, at).start()

    return [going(side, at) for side in range(2) for at in range(CHUNKS // 2)]


def attend_kernel(
    second, core_ref, begin_ref, note_ref, low_ref, tops_ref, kv_ref, q_ref, out_ref,
    kv_in, q_in, place_ref, qs_ref, os_ref, built, turn_c, turn_s, q_mark, kt, vv, causal, sems, out_sems,
):
    tabs = turn_c, turn_s, q_mark, kt, vv, causal
    core = core_ref[0]
    arriving = []
    for side in range(2):
        here = kv_ref.at[:, side ^ core, : 2 * PER]
        arriving += start([pltpu.make_async_copy(here, kv_in.at[side], sems.at[0, side])])
    for side in range(2):
        here = q_ref.at[:, side] if second else q_ref.at[:, side ^ core, 2 * PER : (2 + PART) * PER]
        arriving += start([pltpu.make_async_copy(here, q_in.at[side], sems.at[1, side])])
    wait(arriving[:2])
    prepare(begin_ref, kv_in, note_ref, low_ref, tops_ref, tabs, place_ref)
    wait(arriving[2:])
    take_queries(q_in, 0, tabs, qs_ref)
    attend_blocks(tabs, qs_ref, os_ref)
    targets = [out_ref.at[:, side ^ core] if second else out_ref.at[:, side] for side in range(2)]
    wait(give_back(os_ref, built, targets, out_sems))


def attend(second, core, begin, note, kv, queries):
    low, tops = turn_table()
    pairs = PART * GROUP * GROUP * 36 // 64
    return pl.pallas_call(
        functools.partial(attend_kernel, second),
        in_specs=[smem(), smem(), vmem(), vmem(), vmem(), anywhere(), anywhere()],
        out_specs=anywhere(),
        out_shape=jax.ShapeDtypeStruct((CHIPS, 2, PART, PER, HD), bf16),
        scratch_shapes=[
            pltpu.VMEM((2, CHIPS, 2 * PER, HD), bf16),
            pltpu.VMEM((2, CHIPS, PART * PER, HD), bf16),
            pltpu.VMEM((GROUP, HD), f32),
            pltpu.VMEM((SEQ, PART * ROWS, 2 * HD), bf16),
            pltpu.VMEM((SEQ, PART * ROWS, HD), bf16),
            pltpu.VMEM((CHUNKS, 16, PART, PER, HD), bf16),
            pltpu.VMEM((GROUP, HD), f32),
            pltpu.VMEM((GROUP, HD), f32),
            pltpu.VMEM((GROUP, HD), bf16),
            pltpu.VMEM((2 * HD, GROUP), bf16),
            pltpu.VMEM((GROUP, 2 * HD), bf16),
            pltpu.VMEM((GROUP, ROWS), f32),
            pltpu.SemaphoreType.DMA((2, 2)),
            pltpu.SemaphoreType.DMA((CHUNKS,)),
        ],
        compiler_params=params(60),
        cost_estimate=work(pairs * 4 * 256, 16 * MIB, pairs),
        name="attend",
    )(core, begin, note, jnp.asarray(low), jnp.asarray(tops), kv, queries)


def exchange(x, axes):
    return lax.all_to_all(x, axes, split_axis=0, concat_axis=0, tiled=True)


def swap(x):
    return lax.ppermute(x, "core", [(0, 1), (1, 0)])


def document_begins(note):
    group = lax.axis_index("dp")
    units = lax.dynamic_slice(note, (COLS * group, 0, PER), (COLS, 2, 2)).reshape(16)
    return jnp.sum((units[None, :] < units[:, None]).astype(jnp.int32), axis=1)


def per_device(queries, keys, values, plan, segment_ids):
    core = lax.axis_index("core").astype(jnp.int32)
    cores = core.reshape(1)
    send_0, perm, back = first_pack(plan, segment_ids, keys, values, queries)
    keep, give = second_pack(cores, perm, queries)
    send_1 = place(keep, swap(give))
    got_0 = exchange(send_0, FLAT)
    got_0, send_1 = lax.optimization_barrier((got_0, send_1))
    got_0 = got_0.reshape(CHIPS, 2, -1, HD)
    got_1 = exchange(send_1, CHIP_AXES)
    note = got_0[:, :, got_0.shape[2] - NOTE].astype(f32)
    sides = jnp.where(core == 0, note, note[:, ::-1])
    sides = jnp.concatenate([sides[:, 0], sides[:, 1]], axis=0)
    begin = document_begins(note)
    out_0 = attend(False, cores, begin, sides, got_0, got_0)
    got_1, out_0 = lax.optimization_barrier((got_1, out_0))
    home_0 = exchange(out_0, CHIP_AXES)
    out_1 = attend(True, cores, begin, sides, got_0, got_1)
    home_0, out_1 = lax.optimization_barrier((home_0, out_1))
    home_1 = exchange(out_1.reshape(DEVICES, PART, PER, HD), FLAT)
    result = unpack(cores, back, [home_0, swap(home_0[:, 1])], 0, None)
    home_1, result = lax.optimization_barrier((home_1, result))
    home_1 = home_1.reshape(CHIPS, 2, PART, PER, HD)
    return unpack(jnp.zeros_like(cores), back, [home_1, home_1], 1, result)


def solution(mesh):
    chips = Mesh(mesh.devices.reshape(GROUPS, COLS, 2), FLAT)
    return jax.shard_map(
        per_device,
        mesh=chips,
        in_specs=(
            P(FLAT, None),
            P(FLAT, None),
            P(FLAT, None),
            P(FLAT),
            P(FLAT),
        ),
        out_specs=P(FLAT, None),
        check_vma=False,
    )
```

```python
import functools

import jax
import jax.numpy as jnp
import numpy as np
from jax import lax
from jax.experimental import pallas as pl
from jax.experimental.pallas import tpu as pltpu
from jax.sharding import Mesh
from jax.sharding import PartitionSpec as P

H = 64
KVH = 8
HD = 128
ROWS = 256
SEQ = 8
GROUPS = 16
COLS = SEQ // 2
CHIPS = GROUPS * COLS
DEVICES = 2 * CHIPS
PER = ROWS // GROUPS
GROUP = SEQ * ROWS
PER_KV = H // KVH
CHUNKS = GROUP // ROWS
PART = 4
NOTE = 8
WIDE = PART * HD
BIG = 1e30
theta_base = 500000.0
MIB = 1024 * 1024

FLAT = ("dp", "z", "core")
CHIP_AXES = ("dp", "z")

f32 = jnp.float32
bf16 = jnp.bfloat16


def params(mib):
    return pltpu.CompilerParams(vmem_limit_bytes=mib * MIB)


def dot(a, b):
    return jnp.dot(a, b, preferred_element_type=f32)


def iota(shape, axis):
    return lax.broadcasted_iota(jnp.int32, shape, axis)


def order(plan_ref, ids_ref, perm_ref, back_ref):
    square = (ROWS, ROWS)
    wide = jnp.broadcast_to(plan_ref[...].astype(f32), square)
    tall = wide.T
    rank_row = jnp.sum((tall < wide).astype(f32), axis=0, keepdims=True).astype(jnp.int32)
    rank_col = jnp.sum((wide < tall).astype(f32), axis=1, keepdims=True).astype(jnp.int32)
    hit = rank_row == iota(square, 0)
    perm_ref[...] = hit.astype(bf16)
    back_ref[...] = (rank_col == iota(square, 1)).astype(bf16)
    ordered = jnp.sum(jnp.where(hit, wide, 0.0), axis=1, keepdims=True).astype(jnp.int32)
    place = (ordered & (ROWS - 1)).astype(f32)
    tall_shape = (ROWS, HD)
    laid = jnp.where((iota(tall_shape, 0) & (PER - 1)) == iota(tall_shape, 1), place, 0.0).astype(bf16)
    flat = (GROUPS * NOTE, ROWS)
    pick = ((iota(flat, 0) >> 3) == (iota(flat, 1) >> 4)).astype(bf16)
    lane = iota((GROUPS * NOTE, HD), 1)
    ids = ids_ref[...].astype(f32)
    note = jnp.where(lane == PER, ids[:, :1], dot(pick, laid))
    return jnp.where(lane == PER + 1, ids[:, ROWS - 1 :], note).astype(bf16)


def lanes(start, width):
    return pl.ds(pl.multiple_of(start, HD), width)


def start(copies):
    for copy in copies:
        copy.start()
    return copies


def wait(copies):
    for copy in copies:
        copy.wait()


def first_pack_kernel(
    plan_ref, ids_ref, k_ref, v_ref, q_ref, out_ref, perm_out, back_out,
    plan_in, ids_in, buffer, built, perm_ref, back_ref, sems, more_sems,
):
    early = start([
        pltpu.make_async_copy(plan_ref, plan_in, more_sems.at[0]),
        pltpu.make_async_copy(ids_ref, ids_in, more_sems.at[1]),
    ])
    copies = []
    for slot in range(SEQ):
        places = (
            (k_ref, slot * HD, 0, HD),
            (v_ref, slot * HD, HD, HD),
            (q_ref, slot * PER_KV * HD, 2 * HD, WIDE),
        )
        copies.append(start([
            pltpu.make_async_copy(
                ref.at[:, pl.ds(here, width)], buffer.at[slot, :, pl.ds(there, width)], sems.at[number, slot]
            )
            for number, (ref, here, there, width) in enumerate(places)
        ]))
    wait(early)
    note = order(plan_in, ids_in, perm_ref, back_ref).reshape(GROUPS, NOTE, HD)
    leaving = start([
        pltpu.make_async_copy(perm_ref, perm_out, more_sems.at[2]),
        pltpu.make_async_copy(back_ref, back_out, more_sems.at[3]),
    ])
    length = (PART + 2) * PER
    for z in range(COLS):
        for c in range(2):
            built[2 * z + c, :, length:, :] = note
    for low in range(0, SEQ, 4):
        for slot in range(low, low + 4):
            wait(copies[slot])
        for slot in range(low, low + 4):
            moved = dot(perm_ref[...], buffer[slot]).astype(bf16)
            for j in range(PART + 2):
                built[slot, :, j * PER : j * PER + PER, :] = moved[:, j * HD : j * HD + HD].reshape(GROUPS, PER, HD)
            leaving += start([pltpu.make_async_copy(built.at[slot], out_ref.at[:, slot], sems.at[3, slot])])
    wait(leaving)


def second_pack_kernel(core_ref, perm_ref, q_ref, keep_ref, give_ref, perm_in, buffer, built, sems, more_sems):
    early = start([pltpu.make_async_copy(perm_ref, perm_in, more_sems.at[0])])
    copies = []
    for z in range(COLS):
        for r in range(2):
            head = 2 * z + (r ^ core_ref[0])
            slot = 2 * z + r
            copies += start([
                pltpu.make_async_copy(
                    q_ref.at[:, lanes(head * (PER_KV * HD) + WIDE, WIDE)], buffer.at[slot], sems.at[0, slot]
                )
            ])
    wait(early)
    leaving = []
    for low in range(0, SEQ, 4):
        wait(copies[low : low + 4])
        for slot in range(low, low + 4):
            moved = dot(perm_in[...], buffer[slot]).astype(bf16)
            for j in range(PART):
                built[slot, :, j * PER : j * PER + PER, :] = moved[:, j * HD : j * HD + HD].reshape(GROUPS, PER, HD)
            z, r = divmod(slot, 2)
            there = keep_ref.at[:, z, 0] if r == 0 else give_ref.at[:, z]
            leaving += start([pltpu.make_async_copy(built.at[slot], there, sems.at[1, slot])])
    wait(leaving)


def lanes(first, width):
    return pl.ds(pl.multiple_of(first, HD), width)


def anywhere():
    return pl.BlockSpec(memory_space=pl.ANY)


def smem():
    return pl.BlockSpec(memory_space=pltpu.SMEM)


def vmem():
    return pl.BlockSpec(memory_space=pltpu.VMEM)


def work(flops, moved, transcendentals=0):
    return pl.CostEstimate(flops=flops, bytes_accessed=moved, transcendentals=transcendentals)


def first_pack(plan, segment_ids, keys, values, queries):
    length = (PART + 2) * PER + NOTE
    square = (ROWS, ROWS)
    out, perm, back = pl.pallas_call(
        first_pack_kernel,
        in_specs=[anywhere()] * 5,
        out_specs=[anywhere()] * 3,
        out_shape=(
            jax.ShapeDtypeStruct((GROUPS, SEQ, length, HD), bf16),
            jax.ShapeDtypeStruct(square, bf16),
            jax.ShapeDtypeStruct(square, bf16),
        ),
        scratch_shapes=[
            pltpu.VMEM((1, ROWS), jnp.int32),
            pltpu.VMEM((1, ROWS), jnp.int32),
            pltpu.VMEM((SEQ, ROWS, (PART + 2) * HD), bf16),
            pltpu.VMEM((SEQ, GROUPS, length, HD), bf16),
            pltpu.VMEM(square, bf16),
            pltpu.VMEM(square, bf16),
            pltpu.SemaphoreType.DMA((4, SEQ)),
            pltpu.SemaphoreType.DMA((4,)),
        ],
        compiler_params=params(60),
        cost_estimate=work(2 * ROWS * ROWS * SEQ * 768, 4 * ROWS * SEQ * 768),
        name="first_pack",
    )(plan.reshape(1, ROWS), segment_ids.reshape(1, ROWS), keys, values, queries)
    return out.reshape(DEVICES, length, HD), perm, back


def second_pack(core, perm, queries):
    length = PART * PER
    keep, give = pl.pallas_call(
        second_pack_kernel,
        in_specs=[smem(), anywhere(), anywhere()],
        out_specs=[anywhere()] * 2,
        out_shape=[
            jax.ShapeDtypeStruct((GROUPS, COLS, 2, length, HD), bf16),
            jax.ShapeDtypeStruct((GROUPS, COLS, length, HD), bf16),
        ],
        scratch_shapes=[
            pltpu.VMEM((ROWS, ROWS), bf16),
            pltpu.VMEM((SEQ, ROWS, WIDE), bf16),
            pltpu.VMEM((SEQ, GROUPS, PART * PER, HD), bf16),
            pltpu.SemaphoreType.DMA((2, SEQ)),
            pltpu.SemaphoreType.DMA((1,)),
        ],
        compiler_params=params(60),
        cost_estimate=work(2 * ROWS * ROWS * SEQ * WIDE, 4 * ROWS * SEQ * WIDE),
        name="second_pack",
    )(core, perm, queries)
    return keep.reshape(CHIPS, 2, length, HD), give.reshape(CHIPS, length, HD)


def place_kernel(taken_ref, keep_ref, out_ref, buffer, sems):
    step = CHIPS // 4
    arriving, leaving = [], []
    for i in range(4):
        here = pl.ds(i * step, step)
        arriving += start([pltpu.make_async_copy(taken_ref.at[here], buffer.at[here], sems.at[0, i])])
        leaving.append(pltpu.make_async_copy(buffer.at[here], out_ref.at[here, 1], sems.at[1, i]))
    for coming, going in zip(arriving, leaving):
        coming.wait()
        going.start()
    wait(leaving)


def place(keep, taken):
    return pl.pallas_call(
        place_kernel,
        in_specs=[anywhere()] * 2,
        out_specs=anywhere(),
        out_shape=jax.ShapeDtypeStruct(keep.shape, keep.dtype),
        scratch_shapes=[pltpu.VMEM(taken.shape, taken.dtype), pltpu.SemaphoreType.DMA((2, 4))],
        input_output_aliases={1: 0},
        compiler_params=params(16),
        cost_estimate=work(0, 2 * taken.size * 2),
        name="place",
    )(taken, keep)


def unpack_kernel(part, core_ref, back_ref, *refs):
    sources = refs[:2]
    out_ref, back_in, buffer, built, sems, more_sems = refs[-6:]
    early = start([pltpu.make_async_copy(back_ref, back_in, more_sems.at[0])])
    arriving, leaving = [], []
    for r in range(2):
        for z in range(COLS):
            slot = r * COLS + z
            here = sources[r].at[:, z, r] if len(sources[r].shape) == 6 else sources[r].at[:, z]
            arriving += start([pltpu.make_async_copy(here, buffer.at[slot], sems.at[0, slot])])
    wait(early)
    for r in range(2):
        wait(arriving[r * COLS : r * COLS + COLS])
        for z in range(COLS):
            slot = r * COLS + z
            heads = [buffer[slot, :, j].reshape(ROWS, HD) for j in range(PART)]
            built[slot] = dot(back_in[...], jnp.concatenate(heads, axis=1)).astype(bf16)
            here = lanes((2 * z + (r ^ core_ref[0])) * (PER_KV * HD) + part * WIDE, WIDE)
            leaving += start([pltpu.make_async_copy(built.at[slot], out_ref.at[:, here], sems.at[1, slot])])
    wait(leaving)


def unpack(core, back, homes, part, into):
    more = [] if into is None else [into]
    return pl.pallas_call(
        functools.partial(unpack_kernel, part),
        in_specs=[smem()] + [anywhere()] * (3 + len(more)),
        out_specs=anywhere(),
        out_shape=jax.ShapeDtypeStruct((ROWS, H * HD), bf16),
        scratch_shapes=[
            pltpu.VMEM((ROWS, ROWS), bf16),
            pltpu.VMEM((SEQ, GROUPS, PART, PER, HD), bf16),
            pltpu.VMEM((SEQ, ROWS, WIDE), bf16),
            pltpu.SemaphoreType.DMA((2, SEQ)),
            pltpu.SemaphoreType.DMA((1,)),
        ],
        input_output_aliases={} if into is None else {4: 0},
        compiler_params=params(16),
        cost_estimate=work(2 * ROWS * ROWS * SEQ * WIDE, 4 * ROWS * SEQ * WIDE),
        name="unpack_rows",
    )(core, back, *[home.reshape(GROUPS, COLS, *home.shape[1:]) for home in homes], *more)


def turn_table():
    freqs = np.float32(theta_base) ** (np.float32(-2.0) * np.arange(HD // 2, dtype=np.float32) / np.float32(HD))
    freqs = freqs.astype(np.float64)
    low = np.arange(HD, dtype=np.float64)[:, None] * freqs[None, :]
    table = np.concatenate([np.cos(low), np.sin(low)], axis=1)
    terms = []
    for _ in range(3):
        term = table.astype(jnp.bfloat16)
        terms.append(term)
        table = table - term.astype(np.float64)
    high = 128.0 * np.arange(16, dtype=np.float64)[:, None] * freqs[None, :]
    c, s = np.cos(high), np.sin(high)
    tops = np.stack([np.concatenate(pair, axis=1) for pair in ((c, -s), (-s, c), (-c, s))])
    return np.concatenate(terms, axis=1), tops.astype(np.float32)


def source(j):
    return ((j >> 1) & 15) * 16 + 2 * (j >> 5) + (j & 1)


def chunk_of(x_ref, chunk, number):
    side = chunk // (CHUNKS // 2)
    loaders = pl.ds(chunk % (CHUNKS // 2) * 16, 16)
    return x_ref[side, loaders, number * PER : number * PER + PER].reshape(ROWS, HD)


def chunk_rows(chunk, s):
    return pl.ds(s * ROWS + chunk * 32, 32)


def settle():
    square = (ROWS, ROWS)
    return (source(iota(square, 0)) == iota(square, 1)).astype(bf16)


def unsettle():
    square = (ROWS, ROWS)
    return (source(iota(square, 1)) == iota(square, 0)).astype(bf16)


def prepare(begin_ref, x_ref, note_ref, low_ref, tops_ref, tabs, place_ref):
    turn_c_ref, turn_s_ref, q_mark_ref, kt_ref, vv_ref, causal_ref = tabs
    perm = settle()
    strip = (ROWS, 16)
    loader = (((iota(strip, 0) >> 1) & 15) == iota(strip, 1)).astype(bf16)
    wide = (ROWS, HD)
    row, lane = iota(wide, 0), iota(wide, 1)
    slot = lane == 2 * (row >> 5) + (row & 1)
    ones = jnp.ones((HD, HD), bf16)
    lane = iota((32, HD), 1)
    for chunk in range(CHUNKS):
        notes = note_ref[pl.ds(chunk * 16, 16), :]
        spread = dot(loader, notes.astype(bf16))
        place = dot(jnp.where(slot, spread, 0.0).astype(bf16), ones)
        low = (place.astype(jnp.int32) & (HD - 1)) == iota(wide, 1)
        parts = dot(low.astype(bf16), low_ref[...])
        here = parts[:, :HD] + (parts[:, HD : 2 * HD] + parts[:, 2 * HD :])
        swapped = pltpu.roll(here, HD // 2, 1)
        both = dot(perm, jnp.concatenate([chunk_of(x_ref, chunk, 0), chunk_of(x_ref, chunk, 1)], axis=1))
        keys, values = both[:, :HD], both[:, HD:].astype(bf16)
        keys_swapped = pltpu.roll(keys, HD // 2, 1)
        for s in range(SEQ):
            piece = slice(s * 32, s * 32 + 32)
            at = chunk_rows(chunk, s)
            same = pl.ds(chunk * ROWS + s * 32, 32)
            mine = place[piece, :]
            place_ref[at, :] = mine
            first = mine < float(HD)
            begins = begin_ref[2 * s], begin_ref[2 * s + 1]
            gaps = 2 * s - begins[0], 2 * s + 1 - begins[1]
            top = [jnp.where(first, tops_ref[i, pl.ds(gaps[0], 1), :], tops_ref[i, pl.ds(gaps[1], 1), :]) for i in range(3)]
            turn_c = here[piece, :] * top[0] + swapped[piece, :] * top[1]
            turn_s = here[piece, :] * top[1] + swapped[piece, :] * top[2]
            turn_c_ref[same, :] = turn_c
            turn_s_ref[same, :] = turn_s
            q_mark_ref[at, :] = jnp.where(lane < jnp.where(first, begins[0], begins[1]), -BIG, 0.0).astype(bf16)
            turned = keys[piece, :] * turn_c + keys_swapped[piece, :] * turn_s
            vv_ref[at, HD:] = turned.astype(bf16)
            vv_ref[at, :HD] = values[piece, :]

    for s in range(SEQ):
        at = slice(s * ROWS, s * ROWS + ROWS)
        kt_ref[:HD, at] = vv_ref[at, HD:].astype(f32).T.astype(bf16)
        across = place_ref[at, :].T
        unit = jnp.where(across < float(HD), 2 * s, 2 * s + 1)
        kt_ref[HD:, at] = (unit == iota((HD, ROWS), 0)).astype(bf16)
        down = jnp.concatenate([place_ref[at, :], place_ref[at, :]], axis=1)
        causal_ref[at, :] = jnp.where(across[:1, :] <= down, 0.0, -BIG)
    vv_ref[:, HD:] = jnp.ones((GROUP, HD), bf16)


def take_queries(x_ref, first, tabs, qs_ref):
    turn_c_ref, turn_s_ref, q_mark_ref = tabs[:3]
    perm = settle()
    for chunk in range(CHUNKS):
        moved = dot(perm, jnp.concatenate([chunk_of(x_ref, chunk, first + h) for h in range(PART)], axis=1))
        same = pl.ds(chunk * ROWS, ROWS)
        turn_c, turn_s = turn_c_ref[same, :], turn_s_ref[same, :]
        for h in range(PART):
            one = moved[:, h * HD : h * HD + HD]
            one = (one * turn_c + pltpu.roll(one, HD // 2, 1) * turn_s).astype(bf16)
            for s in range(SEQ):
                qs_ref[s, chunk_rows(chunk, h), :HD] = one[s * 32 : s * 32 + 32]

    for s in range(SEQ):
        for h in range(PART):
            qs_ref[s, h * ROWS : h * ROWS + ROWS, HD:] = q_mark_ref[s * ROWS : s * ROWS + ROWS, :]


def attend_blocks(tabs, qs_ref, os_ref):
    kt_ref, vv_ref, causal_ref = tabs[3:]
    factor = (HD ** -0.5) * 1.4426950408889634

    def scores(s, rows):
        return dot(qs_ref[s, rows, :], kt_ref[:, : s * ROWS + ROWS])

    def finish(s, rows, score):
        here = slice(s * ROWS, s * ROWS + ROWS)
        diagonal = score[:, s * ROWS :] + causal_ref[here, :]
        score = diagonal if s == 0 else jnp.concatenate([score[:, : s * ROWS], diagonal], axis=1)
        peak = jnp.max(score, axis=1, keepdims=True)
        weight = jnp.exp2((score - peak) * factor).astype(bf16)
        mixed = dot(weight, vv_ref[: s * ROWS + ROWS, :])
        os_ref[s, rows, :] = (mixed[:, :HD] / mixed[:, HD:]).astype(bf16)

    @pl.loop(0, PART // 2)
    def _(pair):
        rows = [pl.ds(pl.multiple_of((2 * pair + i) * ROWS, ROWS), ROWS) for i in range(2)]
        items = [(s, rows[i]) for s in range(SEQ) for i in range(2)]
        score = scores(*items[0])
        for number, item in enumerate(items):
            following = scores(*items[number + 1]) if number + 1 < len(items) else None
            finish(*item, score)
            score = following


def give_back(os_ref, built, targets, sems):
    perm = unsettle()

    def going(side, at):
        chunk = side * (CHUNKS // 2) + at
        there = targets[side].at[pl.ds(at * 16, 16)]
        return pltpu.make_async_copy(built.at[chunk], there, sems.at[chunk])

    for side in range(2):
        for at in range(CHUNKS // 2):
            chunk = side * (CHUNKS // 2) + at
            heads = []
            for h in range(PART):
                heads.append(jnp.concatenate([os_ref[s, chunk_rows(chunk, h), :] for s in range(SEQ)], axis=0))
            moved = dot(perm, jnp.concatenate(heads, axis=1)).astype(bf16)
            for h in range(PART):
                built[chunk, :, h] = moved[:, h * HD : h * HD + HD].reshape(16, PER, HD)
            going(side, at).start()

    return [going(side, at) for side in range(2) for at in range(CHUNKS // 2)]


def attend_kernel(
    second, core_ref, begin_ref, note_ref, low_ref, tops_ref, kv_ref, q_ref, *refs,
):
    outs, refs = refs[: 1 + second], refs[1 + second :]
    kv_in, q_in, place_ref, qs_ref, os_ref, built, turn_c, turn_s, q_mark, kt, vv, causal, sems, out_sems = refs
    tabs = turn_c, turn_s, q_mark, kt, vv, causal
    core = core_ref[0]
    arriving = []
    for side in range(2):
        here = kv_ref.at[:, side ^ core, : 2 * PER]
        arriving += start([pltpu.make_async_copy(here, kv_in.at[side], sems.at[0, side])])
    for side in range(2):
        here = q_ref.at[:, side] if second else q_ref.at[:, side ^ core, 2 * PER : (2 + PART) * PER]
        arriving += start([pltpu.make_async_copy(here, q_in.at[side], sems.at[1, side])])
    wait(arriving[:2])
    prepare(begin_ref, kv_in, note_ref, low_ref, tops_ref, tabs, place_ref)
    wait(arriving[2:])
    take_queries(q_in, 0, tabs, qs_ref)
    attend_blocks(tabs, qs_ref, os_ref)
    targets = (outs[0].at[:, 0], outs[1]) if second else [outs[0].at[:, side ^ core] for side in range(2)]
    wait(give_back(os_ref, built, targets, out_sems))


def attend(second, core, begin, note, kv, queries):
    low, tops = turn_table()
    pairs = PART * GROUP * GROUP * 36 // 64
    return pl.pallas_call(
        functools.partial(attend_kernel, second),
        in_specs=[smem(), smem(), vmem(), vmem(), vmem(), anywhere(), anywhere()],
        out_specs=[anywhere()] * (1 + second),
        out_shape=[
            jax.ShapeDtypeStruct((CHIPS, 2, PART, PER, HD), bf16),
            jax.ShapeDtypeStruct((CHIPS, PART, PER, HD), bf16),
        ][: 1 + second],
        scratch_shapes=[
            pltpu.VMEM((2, CHIPS, 2 * PER, HD), bf16),
            pltpu.VMEM((2, CHIPS, PART * PER, HD), bf16),
            pltpu.VMEM((GROUP, HD), f32),
            pltpu.VMEM((SEQ, PART * ROWS, 2 * HD), bf16),
            pltpu.VMEM((SEQ, PART * ROWS, HD), bf16),
            pltpu.VMEM((CHUNKS, 16, PART, PER, HD), bf16),
            pltpu.VMEM((GROUP, HD), f32),
            pltpu.VMEM((GROUP, HD), f32),
            pltpu.VMEM((GROUP, HD), bf16),
            pltpu.VMEM((2 * HD, GROUP), bf16),
            pltpu.VMEM((GROUP, 2 * HD), bf16),
            pltpu.VMEM((GROUP, ROWS), f32),
            pltpu.SemaphoreType.DMA((2, 2)),
            pltpu.SemaphoreType.DMA((CHUNKS,)),
        ],
        compiler_params=params(60),
        cost_estimate=work(pairs * 4 * 256, 16 * MIB, pairs),
        name="attend",
    )(core, begin, note, jnp.asarray(low), jnp.asarray(tops), kv, queries)


def exchange(x, axes):
    return lax.all_to_all(x, axes, split_axis=0, concat_axis=0, tiled=True)


def swap(x):
    return lax.ppermute(x, "core", [(0, 1), (1, 0)])


def document_begins(note):
    group = lax.axis_index("dp")
    units = lax.dynamic_slice(note, (COLS * group, 0, PER), (COLS, 2, 2)).reshape(16)
    return jnp.sum((units[None, :] < units[:, None]).astype(jnp.int32), axis=1)


def per_device(queries, keys, values, plan, segment_ids):
    core = lax.axis_index("core").astype(jnp.int32)
    cores = core.reshape(1)
    send_0, perm, back = first_pack(plan, segment_ids, keys, values, queries)
    keep, give = second_pack(cores, perm, queries)
    send_1 = place(keep, swap(give))
    got_0 = exchange(send_0, FLAT)
    got_0, send_1 = lax.optimization_barrier((got_0, send_1))
    got_0 = got_0.reshape(CHIPS, 2, -1, HD)
    got_1 = exchange(send_1, CHIP_AXES)
    note = got_0[:, :, got_0.shape[2] - NOTE].astype(f32)
    sides = jnp.where(core == 0, note, note[:, ::-1])
    sides = jnp.concatenate([sides[:, 0], sides[:, 1]], axis=0)
    begin = document_begins(note)
    (out_0,) = attend(False, cores, begin, sides, got_0, got_0)
    got_1, out_0 = lax.optimization_barrier((got_1, out_0))
    home_0 = exchange(out_0.reshape(DEVICES, PART, PER, HD), FLAT).reshape(out_0.shape)
    keep, give = attend(True, cores, begin, sides, got_0, got_1)
    out_1 = place(keep, swap(give))
    home_0, out_1 = lax.optimization_barrier((home_0, out_1))
    home_1 = exchange(out_1, CHIP_AXES)
    result = unpack(jnp.zeros_like(cores), back, [home_0, home_0], 0, None)
    home_1, result = lax.optimization_barrier((home_1, result))
    return unpack(cores, back, [home_1, home_1], 1, result)


def solution(mesh):
    chips = Mesh(mesh.devices.reshape(GROUPS, COLS, 2), FLAT)
    return jax.shard_map(
        per_device,
        mesh=chips,
        in_specs=(
            P(FLAT, None),
            P(FLAT, None),
            P(FLAT, None),
            P(FLAT),
            P(FLAT),
        ),
        out_specs=P(FLAT, None),
        check_vma=False,
    )
```

```python
import functools

import jax
import jax.numpy as jnp
import numpy as np
from jax import lax
from jax.experimental import pallas as pl
from jax.experimental.pallas import tpu as pltpu
from jax.sharding import Mesh
from jax.sharding import PartitionSpec as P

H = 64
KVH = 8
HD = 128
ROWS = 256
SEQ = 8
GROUPS = 16
COLS = SEQ // 2
CHIPS = GROUPS * COLS
DEVICES = 2 * CHIPS
PER = ROWS // GROUPS
GROUP = SEQ * ROWS
PER_KV = H // KVH
CHUNKS = GROUP // ROWS
PART = 4
NOTE = 16
WIDE = PART * HD
BIG = 1e30
theta_base = 500000.0
MIB = 1024 * 1024

FLAT = ("dp", "z", "core")
CHIP_AXES = ("dp", "z")

f32 = jnp.float32
bf16 = jnp.bfloat16


def params(mib):
    return pltpu.CompilerParams(vmem_limit_bytes=mib * MIB)


def dot(a, b):
    return jnp.dot(a, b, preferred_element_type=f32)


def iota(shape, axis):
    return lax.broadcasted_iota(jnp.int32, shape, axis)


def order(plan_ref, ids_ref, perm_ref, back_ref):
    square = (ROWS, ROWS)
    wide = jnp.broadcast_to(plan_ref[...].astype(f32), square)
    tall = wide.T
    rank_row = jnp.sum((tall < wide).astype(f32), axis=0, keepdims=True).astype(jnp.int32)
    rank_col = jnp.sum((wide < tall).astype(f32), axis=1, keepdims=True).astype(jnp.int32)
    hit = rank_row == iota(square, 0)
    perm_ref[...] = hit.astype(bf16)
    back_ref[...] = (rank_col == iota(square, 1)).astype(bf16)
    ordered = jnp.sum(jnp.where(hit, wide, 0.0), axis=1, keepdims=True).astype(jnp.int32)
    place = (ordered & (ROWS - 1)).astype(f32)
    tall_shape = (ROWS, HD)
    laid = jnp.where((iota(tall_shape, 0) & (PER - 1)) == iota(tall_shape, 1), place, 0.0).astype(bf16)
    flat = (GROUPS * NOTE, ROWS)
    pick = ((iota(flat, 0) // NOTE) == (iota(flat, 1) >> 4)).astype(bf16)
    lane = iota((GROUPS * NOTE, HD), 1)
    ids = ids_ref[...].astype(f32)
    note = jnp.where(lane == PER, ids[:, :1], dot(pick, laid))
    return jnp.where(lane == PER + 1, ids[:, ROWS - 1 :], note).astype(bf16)


def lanes(start, width):
    return pl.ds(pl.multiple_of(start, HD), width)


def start(copies):
    for copy in copies:
        copy.start()
    return copies


def wait(copies):
    for copy in copies:
        copy.wait()


def first_pack_kernel(
    plan_ref, ids_ref, k_ref, v_ref, q_ref, out_ref, perm_out, back_out,
    plan_in, ids_in, buffer, built, perm_ref, back_ref, sems, more_sems,
):
    early = start([
        pltpu.make_async_copy(plan_ref, plan_in, more_sems.at[0]),
        pltpu.make_async_copy(ids_ref, ids_in, more_sems.at[1]),
    ])
    copies = []
    for slot in range(SEQ):
        places = (
            (k_ref, slot * HD, 0, HD),
            (v_ref, slot * HD, HD, HD),
            (q_ref, slot * PER_KV * HD, 2 * HD, WIDE),
        )
        copies.append(start([
            pltpu.make_async_copy(
                ref.at[:, pl.ds(here, width)], buffer.at[slot, :, pl.ds(there, width)], sems.at[number, slot]
            )
            for number, (ref, here, there, width) in enumerate(places)
        ]))
    wait(early)
    note = order(plan_in, ids_in, perm_ref, back_ref).reshape(GROUPS, NOTE, HD)
    leaving = start([
        pltpu.make_async_copy(perm_ref, perm_out, more_sems.at[2]),
        pltpu.make_async_copy(back_ref, back_out, more_sems.at[3]),
    ])
    length = (PART + 2) * PER
    for z in range(COLS):
        for c in range(2):
            built[2 * z + c, :, length:, :] = note
    for low in range(0, SEQ, 4):
        for slot in range(low, low + 4):
            wait(copies[slot])
        for slot in range(low, low + 4):
            moved = dot(perm_ref[...], buffer[slot]).astype(bf16)
            for j in range(PART + 2):
                built[slot, :, j * PER : j * PER + PER, :] = moved[:, j * HD : j * HD + HD].reshape(GROUPS, PER, HD)
            leaving += start([pltpu.make_async_copy(built.at[slot], out_ref.at[:, slot], sems.at[3, slot])])
    wait(leaving)


def second_pack_kernel(core_ref, perm_ref, q_ref, keep_ref, give_ref, perm_in, buffer, built, sems, more_sems):
    early = start([pltpu.make_async_copy(perm_ref, perm_in, more_sems.at[0])])
    copies = []
    for z in range(COLS):
        for r in range(2):
            head = 2 * z + (r ^ core_ref[0])
            slot = 2 * z + r
            copies += start([
                pltpu.make_async_copy(
                    q_ref.at[:, lanes(head * (PER_KV * HD) + WIDE, WIDE)], buffer.at[slot], sems.at[0, slot]
                )
            ])
    wait(early)
    leaving = []
    for low in range(0, SEQ, 4):
        wait(copies[low : low + 4])
        for slot in range(low, low + 4):
            moved = dot(perm_in[...], buffer[slot]).astype(bf16)
            for j in range(PART):
                built[slot, :, j * PER : j * PER + PER, :] = moved[:, j * HD : j * HD + HD].reshape(GROUPS, PER, HD)
            z, r = divmod(slot, 2)
            there = keep_ref.at[:, z, 0] if r == 0 else give_ref.at[:, z]
            leaving += start([pltpu.make_async_copy(built.at[slot], there, sems.at[1, slot])])
    wait(leaving)


def lanes(first, width):
    return pl.ds(pl.multiple_of(first, HD), width)


def anywhere():
    return pl.BlockSpec(memory_space=pl.ANY)


def smem():
    return pl.BlockSpec(memory_space=pltpu.SMEM)


def vmem():
    return pl.BlockSpec(memory_space=pltpu.VMEM)


def work(flops, moved, transcendentals=0):
    return pl.CostEstimate(flops=flops, bytes_accessed=moved, transcendentals=transcendentals)


def first_pack(plan, segment_ids, keys, values, queries):
    length = (PART + 2) * PER + NOTE
    square = (ROWS, ROWS)
    out, perm, back = pl.pallas_call(
        first_pack_kernel,
        in_specs=[anywhere()] * 5,
        out_specs=[anywhere()] * 3,
        out_shape=(
            jax.ShapeDtypeStruct((GROUPS, SEQ, length, HD), bf16),
            jax.ShapeDtypeStruct(square, bf16),
            jax.ShapeDtypeStruct(square, bf16),
        ),
        scratch_shapes=[
            pltpu.VMEM((1, ROWS), jnp.int32),
            pltpu.VMEM((1, ROWS), jnp.int32),
            pltpu.VMEM((SEQ, ROWS, (PART + 2) * HD), bf16),
            pltpu.VMEM((SEQ, GROUPS, length, HD), bf16),
            pltpu.VMEM(square, bf16),
            pltpu.VMEM(square, bf16),
            pltpu.SemaphoreType.DMA((4, SEQ)),
            pltpu.SemaphoreType.DMA((4,)),
        ],
        compiler_params=params(60),
        cost_estimate=work(2 * ROWS * ROWS * SEQ * 768, 4 * ROWS * SEQ * 768),
        name="first_pack",
    )(plan.reshape(1, ROWS), segment_ids.reshape(1, ROWS), keys, values, queries)
    return out.reshape(DEVICES, length, HD), perm, back


def second_pack(core, perm, queries):
    length = PART * PER
    keep, give = pl.pallas_call(
        second_pack_kernel,
        in_specs=[smem(), anywhere(), anywhere()],
        out_specs=[anywhere()] * 2,
        out_shape=[
            jax.ShapeDtypeStruct((GROUPS, COLS, 2, length, HD), bf16),
            jax.ShapeDtypeStruct((GROUPS, COLS, length, HD), bf16),
        ],
        scratch_shapes=[
            pltpu.VMEM((ROWS, ROWS), bf16),
            pltpu.VMEM((SEQ, ROWS, WIDE), bf16),
            pltpu.VMEM((SEQ, GROUPS, PART * PER, HD), bf16),
            pltpu.SemaphoreType.DMA((2, SEQ)),
            pltpu.SemaphoreType.DMA((1,)),
        ],
        compiler_params=params(60),
        cost_estimate=work(2 * ROWS * ROWS * SEQ * WIDE, 4 * ROWS * SEQ * WIDE),
        name="second_pack",
    )(core, perm, queries)
    return keep.reshape(CHIPS, 2, length, HD), give.reshape(CHIPS, length, HD)


def place_kernel(taken_ref, keep_ref, out_ref, buffer, sems):
    step = CHIPS // 4
    arriving, leaving = [], []
    for i in range(4):
        here = pl.ds(i * step, step)
        arriving += start([pltpu.make_async_copy(taken_ref.at[here], buffer.at[here], sems.at[0, i])])
        leaving.append(pltpu.make_async_copy(buffer.at[here], out_ref.at[here, 1], sems.at[1, i]))
    for coming, going in zip(arriving, leaving):
        coming.wait()
        going.start()
    wait(leaving)


def place(keep, taken):
    return pl.pallas_call(
        place_kernel,
        in_specs=[anywhere()] * 2,
        out_specs=anywhere(),
        out_shape=jax.ShapeDtypeStruct(keep.shape, keep.dtype),
        scratch_shapes=[pltpu.VMEM(taken.shape, taken.dtype), pltpu.SemaphoreType.DMA((2, 4))],
        input_output_aliases={1: 0},
        compiler_params=params(16),
        cost_estimate=work(0, 2 * taken.size * 2),
        name="place",
    )(taken, keep)


def unpack_kernel(part, core_ref, back_ref, *refs):
    sources = refs[:2]
    out_ref, back_in, buffer, built, sems, more_sems = refs[-6:]
    early = start([pltpu.make_async_copy(back_ref, back_in, more_sems.at[0])])
    arriving, leaving = [], []
    for r in range(2):
        for z in range(COLS):
            slot = r * COLS + z
            arriving += start([pltpu.make_async_copy(sources[r].at[:, z, r], buffer.at[slot], sems.at[0, slot])])
    wait(early)
    for r in range(2):
        wait(arriving[r * COLS : r * COLS + COLS])
        for z in range(COLS):
            slot = r * COLS + z
            heads = [buffer[slot, :, j].reshape(ROWS, HD) for j in range(PART)]
            built[slot] = dot(back_in[...], jnp.concatenate(heads, axis=1)).astype(bf16)
            here = lanes((2 * z + (r ^ core_ref[0])) * (PER_KV * HD) + part * WIDE, WIDE)
            leaving += start([pltpu.make_async_copy(built.at[slot], out_ref.at[:, here], sems.at[1, slot])])
    wait(leaving)


def unpack(core, back, homes, part, into):
    more = [] if into is None else [into]
    return pl.pallas_call(
        functools.partial(unpack_kernel, part),
        in_specs=[smem()] + [anywhere()] * (3 + len(more)),
        out_specs=anywhere(),
        out_shape=jax.ShapeDtypeStruct((ROWS, H * HD), bf16),
        scratch_shapes=[
            pltpu.VMEM((ROWS, ROWS), bf16),
            pltpu.VMEM((SEQ, GROUPS, PART, PER, HD), bf16),
            pltpu.VMEM((SEQ, ROWS, WIDE), bf16),
            pltpu.SemaphoreType.DMA((2, SEQ)),
            pltpu.SemaphoreType.DMA((1,)),
        ],
        input_output_aliases={} if into is None else {4: 0},
        compiler_params=params(16),
        cost_estimate=work(2 * ROWS * ROWS * SEQ * WIDE, 4 * ROWS * SEQ * WIDE),
        name="unpack_rows",
    )(core, back, *[home.reshape(GROUPS, COLS, 2, PART, PER, HD) for home in homes], *more)


def turn_table():
    freqs = np.float32(theta_base) ** (np.float32(-2.0) * np.arange(HD // 2, dtype=np.float32) / np.float32(HD))
    freqs = freqs.astype(np.float64)
    low = np.arange(HD, dtype=np.float64)[:, None] * freqs[None, :]
    table = np.concatenate([np.cos(low), np.sin(low)], axis=1)
    terms = []
    for _ in range(3):
        term = table.astype(jnp.bfloat16)
        terms.append(term)
        table = table - term.astype(np.float64)
    high = 128.0 * np.arange(16, dtype=np.float64)[:, None] * freqs[None, :]
    c, s = np.cos(high), np.sin(high)
    tops = np.stack([np.concatenate(pair, axis=1) for pair in ((c, -s), (-s, c), (-c, s))])
    return np.concatenate(terms, axis=1), tops.astype(np.float32)


def source(j):
    return ((j >> 1) & 15) * 16 + 2 * (j >> 5) + (j & 1)


def chunk_of(x_ref, chunk, number):
    side = chunk // (CHUNKS // 2)
    loaders = pl.ds(chunk % (CHUNKS // 2) * 16, 16)
    return x_ref[side, loaders, number * PER : number * PER + PER].reshape(ROWS, HD)


def chunk_rows(chunk, s):
    return pl.ds(s * ROWS + chunk * 32, 32)


def settle():
    square = (ROWS, ROWS)
    return (source(iota(square, 0)) == iota(square, 1)).astype(bf16)


def unsettle():
    square = (ROWS, ROWS)
    return (source(iota(square, 1)) == iota(square, 0)).astype(bf16)


def prepare(begin_ref, x_ref, note_ref, low_ref, tops_ref, tabs, place_ref):
    turn_c_ref, turn_s_ref, q_mark_ref, kt_ref, vv_ref, causal_ref = tabs
    perm = settle()
    strip = (ROWS, 16)
    loader = (((iota(strip, 0) >> 1) & 15) == iota(strip, 1)).astype(bf16)
    wide = (ROWS, HD)
    row, lane = iota(wide, 0), iota(wide, 1)
    slot = lane == 2 * (row >> 5) + (row & 1)
    ones = jnp.ones((HD, HD), bf16)
    lane = iota((32, HD), 1)
    for chunk in range(CHUNKS):
        notes = note_ref[pl.ds(chunk * 16, 16), :]
        spread = dot(loader, notes.astype(bf16))
        place = dot(jnp.where(slot, spread, 0.0).astype(bf16), ones)
        low = (place.astype(jnp.int32) & (HD - 1)) == iota(wide, 1)
        parts = dot(low.astype(bf16), low_ref[...])
        here = parts[:, :HD] + (parts[:, HD : 2 * HD] + parts[:, 2 * HD :])
        swapped = pltpu.roll(here, HD // 2, 1)
        both = dot(perm, jnp.concatenate([chunk_of(x_ref, chunk, 0), chunk_of(x_ref, chunk, 1)], axis=1))
        keys, values = both[:, :HD], both[:, HD:].astype(bf16)
        keys_swapped = pltpu.roll(keys, HD // 2, 1)
        for s in range(SEQ):
            piece = slice(s * 32, s * 32 + 32)
            at = chunk_rows(chunk, s)
            same = pl.ds(chunk * ROWS + s * 32, 32)
            mine = place[piece, :]
            place_ref[at, :] = mine
            first = mine < float(HD)
            begins = begin_ref[2 * s], begin_ref[2 * s + 1]
            gaps = 2 * s - begins[0], 2 * s + 1 - begins[1]
            top = [jnp.where(first, tops_ref[i, pl.ds(gaps[0], 1), :], tops_ref[i, pl.ds(gaps[1], 1), :]) for i in range(3)]
            turn_c = here[piece, :] * top[0] + swapped[piece, :] * top[1]
            turn_s = here[piece, :] * top[1] + swapped[piece, :] * top[2]
            turn_c_ref[same, :] = turn_c
            turn_s_ref[same, :] = turn_s
            q_mark_ref[at, :] = jnp.where(lane < jnp.where(first, begins[0], begins[1]), -BIG, 0.0).astype(bf16)
            turned = keys[piece, :] * turn_c + keys_swapped[piece, :] * turn_s
            vv_ref[at, HD:] = turned.astype(bf16)
            vv_ref[at, :HD] = values[piece, :]

    for s in range(SEQ):
        at = slice(s * ROWS, s * ROWS + ROWS)
        kt_ref[:HD, at] = vv_ref[at, HD:].astype(f32).T.astype(bf16)
        across = place_ref[at, :].T
        unit = jnp.where(across < float(HD), 2 * s, 2 * s + 1)
        kt_ref[HD:, at] = (unit == iota((HD, ROWS), 0)).astype(bf16)
        down = jnp.concatenate([place_ref[at, :], place_ref[at, :]], axis=1)
        causal_ref[at, :] = jnp.where(across[:1, :] <= down, 0.0, -BIG)
    vv_ref[:, HD:] = jnp.ones((GROUP, HD), bf16)


def take_queries(x_ref, first, tabs, qs_ref):
    turn_c_ref, turn_s_ref, q_mark_ref = tabs[:3]
    perm = settle()
    for chunk in range(CHUNKS):
        moved = dot(perm, jnp.concatenate([chunk_of(x_ref, chunk, first + h) for h in range(PART)], axis=1))
        same = pl.ds(chunk * ROWS, ROWS)
        turn_c, turn_s = turn_c_ref[same, :], turn_s_ref[same, :]
        for h in range(PART):
            one = moved[:, h * HD : h * HD + HD]
            one = (one * turn_c + pltpu.roll(one, HD // 2, 1) * turn_s).astype(bf16)
            for s in range(SEQ):
                qs_ref[s, chunk_rows(chunk, h), :HD] = one[s * 32 : s * 32 + 32]

    for s in range(SEQ):
        for h in range(PART):
            qs_ref[s, h * ROWS : h * ROWS + ROWS, HD:] = q_mark_ref[s * ROWS : s * ROWS + ROWS, :]


def attend_blocks(tabs, qs_ref, os_ref):
    kt_ref, vv_ref, causal_ref = tabs[3:]
    factor = (HD ** -0.5) * 1.4426950408889634

    def scores(s, rows):
        return dot(qs_ref[s, rows, :], kt_ref[:, : s * ROWS + ROWS])

    def finish(s, rows, score):
        here = slice(s * ROWS, s * ROWS + ROWS)
        diagonal = score[:, s * ROWS :] + causal_ref[here, :]
        score = diagonal if s == 0 else jnp.concatenate([score[:, : s * ROWS], diagonal], axis=1)
        peak = jnp.max(score, axis=1, keepdims=True)
        weight = jnp.exp2((score - peak) * factor).astype(bf16)
        mixed = dot(weight, vv_ref[: s * ROWS + ROWS, :])
        os_ref[s, rows, :] = (mixed[:, :HD] / mixed[:, HD:]).astype(bf16)

    @pl.loop(0, PART // 2)
    def _(pair):
        rows = [pl.ds(pl.multiple_of((2 * pair + i) * ROWS, ROWS), ROWS) for i in range(2)]
        items = [(s, rows[i]) for s in range(SEQ) for i in range(2)]
        score = scores(*items[0])
        for number, item in enumerate(items):
            following = scores(*items[number + 1]) if number + 1 < len(items) else None
            finish(*item, score)
            score = following


def give_back(os_ref, built, targets, sems):
    perm = unsettle()

    def going(side, at):
        chunk = side * (CHUNKS // 2) + at
        there = targets[side].at[pl.ds(at * 16, 16)]
        return pltpu.make_async_copy(built.at[chunk], there, sems.at[chunk])

    for side in range(2):
        for at in range(CHUNKS // 2):
            chunk = side * (CHUNKS // 2) + at
            heads = []
            for h in range(PART):
                heads.append(jnp.concatenate([os_ref[s, chunk_rows(chunk, h), :] for s in range(SEQ)], axis=0))
            moved = dot(perm, jnp.concatenate(heads, axis=1)).astype(bf16)
            for h in range(PART):
                built[chunk, :, h] = moved[:, h * HD : h * HD + HD].reshape(16, PER, HD)
            going(side, at).start()

    return [going(side, at) for side in range(2) for at in range(CHUNKS // 2)]


def attend_kernel(
    second, core_ref, begin_ref, note_ref, low_ref, tops_ref, kv_ref, q_ref, out_ref,
    kv_in, q_in, place_ref, qs_ref, os_ref, built, turn_c, turn_s, q_mark, kt, vv, causal, sems, out_sems,
):
    tabs = turn_c, turn_s, q_mark, kt, vv, causal
    core = core_ref[0]
    arriving = []
    for side in range(2):
        here = kv_ref.at[:, side ^ core, : 2 * PER]
        arriving += start([pltpu.make_async_copy(here, kv_in.at[side], sems.at[0, side])])
    for side in range(2):
        here = q_ref.at[:, side] if second else q_ref.at[:, side ^ core, 2 * PER : (2 + PART) * PER]
        arriving += start([pltpu.make_async_copy(here, q_in.at[side], sems.at[1, side])])
    wait(arriving[:2])
    prepare(begin_ref, kv_in, note_ref, low_ref, tops_ref, tabs, place_ref)
    wait(arriving[2:])
    take_queries(q_in, 0, tabs, qs_ref)
    attend_blocks(tabs, qs_ref, os_ref)
    targets = [out_ref.at[:, side ^ core] if second else out_ref.at[:, side] for side in range(2)]
    wait(give_back(os_ref, built, targets, out_sems))


def attend(second, core, begin, note, kv, queries):
    low, tops = turn_table()
    pairs = PART * GROUP * GROUP * 36 // 64
    return pl.pallas_call(
        functools.partial(attend_kernel, second),
        in_specs=[smem(), smem(), vmem(), vmem(), vmem(), anywhere(), anywhere()],
        out_specs=anywhere(),
        out_shape=jax.ShapeDtypeStruct((CHIPS, 2, PART, PER, HD), bf16),
        scratch_shapes=[
            pltpu.VMEM((2, CHIPS, 2 * PER, HD), bf16),
            pltpu.VMEM((2, CHIPS, PART * PER, HD), bf16),
            pltpu.VMEM((GROUP, HD), f32),
            pltpu.VMEM((SEQ, PART * ROWS, 2 * HD), bf16),
            pltpu.VMEM((SEQ, PART * ROWS, HD), bf16),
            pltpu.VMEM((CHUNKS, 16, PART, PER, HD), bf16),
            pltpu.VMEM((GROUP, HD), f32),
            pltpu.VMEM((GROUP, HD), f32),
            pltpu.VMEM((GROUP, HD), bf16),
            pltpu.VMEM((2 * HD, GROUP), bf16),
            pltpu.VMEM((GROUP, 2 * HD), bf16),
            pltpu.VMEM((GROUP, ROWS), f32),
            pltpu.SemaphoreType.DMA((2, 2)),
            pltpu.SemaphoreType.DMA((CHUNKS,)),
        ],
        compiler_params=params(60),
        cost_estimate=work(pairs * 4 * 256, 16 * MIB, pairs),
        name="attend",
    )(core, begin, note, jnp.asarray(low), jnp.asarray(tops), kv, queries)


def exchange(x, axes):
    return lax.all_to_all(x, axes, split_axis=0, concat_axis=0, tiled=True)


def swap(x):
    return lax.ppermute(x, "core", [(0, 1), (1, 0)])


def document_begins(note):
    group = lax.axis_index("dp")
    units = lax.dynamic_slice(note, (COLS * group, 0, PER), (COLS, 2, 2)).reshape(16)
    return jnp.sum((units[None, :] < units[:, None]).astype(jnp.int32), axis=1)


def per_device(queries, keys, values, plan, segment_ids):
    core = lax.axis_index("core").astype(jnp.int32)
    cores = core.reshape(1)
    send_0, perm, back = first_pack(plan, segment_ids, keys, values, queries)
    keep, give = second_pack(cores, perm, queries)
    send_1 = place(keep, swap(give))
    got_0 = exchange(send_0, FLAT)
    got_0, send_1 = lax.optimization_barrier((got_0, send_1))
    got_0 = got_0.reshape(CHIPS, 2, -1, HD)
    got_1 = exchange(send_1, CHIP_AXES)
    note = got_0[:, :, got_0.shape[2] - NOTE].astype(f32)
    sides = jnp.where(core == 0, note, note[:, ::-1])
    sides = jnp.concatenate([sides[:, 0], sides[:, 1]], axis=0)
    begin = document_begins(note)
    out_0 = attend(False, cores, begin, sides, got_0, got_0)
    got_1, out_0 = lax.optimization_barrier((got_1, out_0))
    home_0 = exchange(out_0, CHIP_AXES)
    out_1 = attend(True, cores, begin, sides, got_0, got_1)
    home_0, out_1 = lax.optimization_barrier((home_0, out_1))
    home_1 = exchange(out_1.reshape(DEVICES, PART, PER, HD), FLAT)
    result = unpack(cores, back, [home_0, swap(home_0)], 0, None)
    home_1, result = lax.optimization_barrier((home_1, result))
    return unpack(jnp.zeros_like(cores), back, [home_1, home_1], 1, result)


def solution(mesh):
    chips = Mesh(mesh.devices.reshape(GROUPS, COLS, 2), FLAT)
    return jax.shard_map(
        per_device,
        mesh=chips,
        in_specs=(
            P(FLAT, None),
            P(FLAT, None),
            P(FLAT, None),
            P(FLAT),
            P(FLAT),
        ),
        out_specs=P(FLAT, None),
        check_vma=False,
    )
```
